32 devices in a mesh: src: 2 (over core), gx: 4 (over z), gy: 4 (over y, x).
Axes of the slice: x: 2, y: 2, z: 4, core: 2. Of those that a mesh axis runs over, the one named last changes fastest.
Arguments:
- forward_state: float32 [4, 6, 64, 16384], P('src', None, 'gx', 'gy'), may hold values from -6 to 6
- adjoint_state: float32 [4, 6, 64, 16384], P('src', None, 'gx', 'gy'), may hold values from -6 to 6
- permittivity: float32 [64, 16384], P('gx', 'gy'), may hold values from 1 to 3
- waveform: float32 [4, 4], P('src'), may hold values from -8 to 8
- source_cell: int32 [4, 3], P('src'), may hold values from 0 to 255, as said below
- block_owner: int32 [16, 64], P('gx', 'gy'), may hold values from -1 to 3, as said below
- block_slot: int32 [16, 64], P('gx', 'gy'), may hold values from -1 to 15, as said below
- owner_rows: int32 [16, 64], P(('gx', 'gy')), may hold values from 0 to 63, as said below
Outputs:
- design_gradient: float32 [1024, 1024], P(('gx', 'gy'), 'src')
The draws below stay inside these ranges and needn't reach their ends.
Inputs may be any that keep to these rules, and one draw needn't show every extreme that they name: `block_owner`: -1 marks a block outside the design region; otherwise the owner lies in the block's own gx row. The design blocks of one device that go to one owner number at most 16, and some device sends exactly 16 to some owner. `block_slot`: -1 exactly where block_owner is -1; the blocks that one device sends to one owner have distinct slots. `owner_rows`: each row is a permutation of 0 to 63. `source_cell`: each row is a cell (x, y, z) of the grid.
All inputs are finite; a program needn't handle non-finite values.
Results may differ from the reference program's by a relative error of at most 0.0003.
Values sent between devices are 32-bit elements; how exact they have to be, the bound alone decides.
A program may use at most 128 MiB of HBM per device.

```python
import math
import jax
import jax.numpy as jnp
from jax import lax

CX = 16
CY = 64
NZ = 64
STEPS = 4
BX = 4
BY = 4
SOURCES = 4
NX = 64
NY = 256
NYZ = 16384
LBX = 4
LBY = 16
LB = 64
NBX = 16
NBY = 64
CAP = 16
PD = 64
ROWS = 1024
N_GX = 4
N_GY = 4


def chosen_row(key):
    return jax.random.randint(jax.random.fold_in(key, 5), (), 0, N_GX)


def design_layout(key):
    devices = N_GX * N_GY
    base_key = jax.random.fold_in(key, 11)
    raw_counts = jax.random.randint(jax.random.fold_in(base_key, 1), (devices,), 0, LB + 1)
    counts = raw_counts * raw_counts // LB
    device_row = jnp.arange(devices) // N_GY
    counts = jnp.where(device_row == chosen_row(key), LB, counts)
    subkeys = jax.random.split(jax.random.fold_in(base_key, 2), devices)
    orders = jax.vmap(lambda single: jax.random.permutation(single, LB))(subkeys)
    position = jnp.argsort(orders, axis=1)
    offsets = jax.random.randint(jax.random.fold_in(base_key, 3), (devices, 1), 0, N_GY)
    column = (jnp.arange(devices) % N_GY)[:, None]
    design = position < counts[:, None]
    owners = jnp.where(design, (column + offsets + position // CAP) % N_GY, -1)
    slots = jnp.where(design, position % CAP, -1)

    def arrange(values):
        return values.reshape(N_GX, N_GY, LBX, LBY).transpose(0, 2, 1, 3).reshape(NBX, NBY).astype(jnp.int32)
    return (arrange(owners), arrange(slots))


def draw_block_owner(key, part):
    return design_layout(key)[0]


def draw_block_slot(key, part):
    return design_layout(key)[1]


def draw_owner_rows(key, part):
    subkeys = jax.random.split(jax.random.fold_in(key, 17), N_GX * N_GY)
    return jax.vmap(lambda single: jax.random.permutation(single, PD))(subkeys).astype(jnp.int32)


def draw_source_cell(key, part):
    base_key = jax.random.fold_in(key, 23)
    picked = jax.random.randint(jax.random.fold_in(base_key, 1), (SOURCES,), 0, N_GY)
    cell_x = chosen_row(key) * CX + jax.random.randint(jax.random.fold_in(base_key, 2), (SOURCES,), 0, CX)
    cell_y = picked * CY + jax.random.randint(jax.random.fold_in(base_key, 3), (SOURCES,), 0, CY)
    cell_z = jax.random.randint(jax.random.fold_in(base_key, 4), (SOURCES,), 0, NZ)
    first = jnp.arange(SOURCES) == 0
    if NY >= NX and NY >= NZ:
        cell_y = jnp.where(first, NY - 1, cell_y)
        cell_z = jnp.where(first, 0, cell_z)
    elif NX >= NZ:
        cell_x = jnp.where(first, NX - 1, cell_x)
        cell_z = jnp.where(first, 0, cell_z)
    else:
        cell_z = jnp.where(first, NZ - 1, cell_z)
        cell_y = jnp.where(first, 0, cell_y)
    return jnp.stack([cell_x, cell_y, cell_z], axis=1).astype(jnp.int32)


def shard_levels(own_key, extent, cuts, smallest, high):
    loudness = 1.0
    for dim, shards_of in cuts:
        heights = jax.random.uniform(jax.random.fold_in(jax.random.fold_in(own_key, 6), dim), (shards_of,), jnp.float32, smallest / len(cuts), high / len(cuts))
        loudness = loudness * jnp.repeat(jnp.exp(heights), extent[dim] // shards_of).reshape((-1,) + (1,) * (len(extent) - 1 - dim))
    return loudness


def centred(own_key, extent, spread, bound, cuts=(), dtype=jnp.bfloat16):
    array = spread * jax.random.normal(own_key, extent, jnp.float32)
    if cuts:
        array = array * shard_levels(own_key, extent, cuts, -0.22, 0.18)
    return jnp.clip(array, -bound, bound).astype(dtype)


def setup_inputs(seed: int = 0) -> dict:
    key_of = jax.random.split(jax.random.key(seed), 9)
    return {
        "forward_state": centred(key_of[0], (SOURCES, 6, NX, NYZ), 1.0, 6.0, ((0, 2), (2, 4), (3, 4)), jnp.float32),
        "adjoint_state": centred(key_of[1], (SOURCES, 6, NX, NYZ), 1.0, 6.0, ((0, 2), (2, 4), (3, 4)), jnp.float32),
        "permittivity": jnp.clip(jnp.exp(math.log(3.0) - 1.0986123 * jax.random.uniform(key_of[2], (NX, NYZ), jnp.float32) ** shard_levels(key_of[2], (NX, NYZ), ((0, 4), (1, 4)), -0.2, 0.2)), 1.0, 3.0),
        "waveform": centred(key_of[3], (SOURCES, STEPS), 2.0, 8.0, ((0, 2),), jnp.float32),
        "source_cell": draw_source_cell(jax.random.fold_in(key_of[8], 71), 0),
        "block_owner": draw_block_owner(jax.random.fold_in(key_of[8], 71), 0),
        "block_slot": draw_block_slot(jax.random.fold_in(key_of[8], 71), 0),
        "owner_rows": draw_owner_rows(jax.random.fold_in(key_of[8], 71), 0),
    }


courant = 0.55


def upper_z(values, z_cells):
    zindex = lax.broadcasted_iota(jnp.int32, values.shape, values.ndim - 1) % z_cells
    shifted = jnp.concatenate([values[..., 1:], jnp.zeros_like(values[..., :1])], axis=-1)
    return jnp.where(zindex == z_cells - 1, jnp.zeros_like(shifted), shifted)


def lower_z(values, z_cells):
    zindex = lax.broadcasted_iota(jnp.int32, values.shape, values.ndim - 1) % z_cells
    shifted = jnp.concatenate([jnp.zeros_like(values[..., :1]), values[..., :-1]], axis=-1)
    return jnp.where(zindex == 0, jnp.zeros_like(shifted), shifted)


def upper_x(values, ghosts):
    return jnp.concatenate([values[..., 1:, :], ghosts], axis=-2)


def lower_x(values, ghosts):
    return jnp.concatenate([ghosts, values[..., :-1, :]], axis=-2)


def upper_y(values, ghosts, z_cells):
    return jnp.concatenate([values[..., z_cells:], ghosts], axis=-1)


def lower_y(values, ghosts, z_cells):
    return jnp.concatenate([ghosts, values[..., :-z_cells]], axis=-1)


def magnetic_update(electric, magnetic, ghost_x, ghost_y, z_cells):
    new_hx = magnetic[0] - courant * ((upper_y(electric[2], ghost_y[1], z_cells) - electric[2]) - (upper_z(electric[1], z_cells) - electric[1]))
    new_hy = magnetic[1] - courant * ((upper_z(electric[0], z_cells) - electric[0]) - (upper_x(electric[2], ghost_x[1]) - electric[2]))
    new_hz = magnetic[2] - courant * ((upper_x(electric[1], ghost_x[0]) - electric[1]) - (upper_y(electric[0], ghost_y[0], z_cells) - electric[0]))
    return (new_hx, new_hy, new_hz)


def electric_update(electric, magnetic, ghost_x, ghost_y, factor, z_cells):
    new_ex = electric[0] + factor * ((magnetic[2] - lower_y(magnetic[2], ghost_y[1], z_cells)) - (magnetic[1] - lower_z(magnetic[1], z_cells)))
    new_ey = electric[1] + factor * ((magnetic[0] - lower_z(magnetic[0], z_cells)) - (magnetic[2] - lower_x(magnetic[2], ghost_x[1])))
    new_ez = electric[2] + factor * ((magnetic[1] - lower_x(magnetic[1], ghost_x[0])) - (magnetic[0] - lower_y(magnetic[0], ghost_y[0], z_cells)))
    return (new_ex, new_ey, new_ez)


def reference(forward_state, adjoint_state, permittivity, waveform, source_cell, block_owner, block_slot, owner_rows):
    factor = courant / permittivity
    cells_x, cells_yz = permittivity.shape
    x_index = lax.broadcasted_iota(jnp.int32, (cells_x, cells_yz), 0)
    yz_index = lax.broadcasted_iota(jnp.int32, (cells_x, cells_yz), 1)
    empty_x = jnp.zeros((1, cells_yz), jnp.float32)
    empty_y = jnp.zeros((cells_x, NZ), jnp.float32)
    ghost_x = (empty_x, empty_x)
    ghost_y = (empty_y, empty_y)

    def advance(electric, magnetic):
        magnetic = magnetic_update(electric, magnetic, ghost_x, ghost_y, NZ)
        electric = electric_update(electric, magnetic, ghost_x, ghost_y, factor, NZ)
        return electric, magnetic

    def one_source(running, inputs):
        forward, adjoint, pulses, location = inputs
        beacon = ((x_index == location[0]) & (yz_index == location[1] * NZ + location[2])).astype(jnp.float32)
        electric = (forward[0], forward[1], forward[2])
        magnetic = (forward[3], forward[4], forward[5])
        increments = []
        for step_index in range(STEPS):
            updated, magnetic = advance(electric, magnetic)
            updated = (updated[0], updated[1], updated[2] + pulses[step_index] * beacon)
            increments.append((updated[0] - electric[0], updated[1] - electric[1], updated[2] - electric[2]))
            electric = updated
        electric = (adjoint[0], adjoint[1], adjoint[2])
        magnetic = (adjoint[3], adjoint[4], adjoint[5])
        density = jnp.zeros((cells_x, cells_yz), jnp.float32)
        for step_index in range(STEPS):
            electric, magnetic = advance(electric, magnetic)
            paired = increments[STEPS - 1 - step_index]
            density = density + (electric[0] * paired[0] + electric[1] * paired[1] + electric[2] * paired[2])
        return running + density, None

    summed, _ = lax.scan(one_source, jnp.zeros((cells_x, cells_yz), jnp.float32), (forward_state, adjoint_state, waveform, source_cell))
    gradient = -summed / permittivity
    blocks = gradient.reshape(NBX, BX, NBY, BY, NZ).transpose(0, 2, 1, 3, 4).reshape(NBX, NBY, BX * BY * NZ)
    row_group = lax.broadcasted_iota(jnp.int32, (NBX, NBY), 0) // LBX
    sender = lax.broadcasted_iota(jnp.int32, (NBX, NBY), 1) // LBY
    owner_safe = jnp.maximum(block_owner, 0)
    slot_safe = jnp.maximum(block_slot, 0)
    owner_device = row_group * N_GY + owner_safe
    target = owner_device * PD + owner_rows[owner_device, sender * CAP + slot_safe]
    target = jnp.where(block_owner >= 0, target, ROWS).astype(jnp.int32)
    placed = jnp.zeros((ROWS, BX * BY * NZ), jnp.float32)
    return placed.at[target.reshape(-1)].set(blocks.reshape(-1, BX * BY * NZ), mode="drop")
```

```python
import functools

import jax
import jax.numpy as jnp
from jax import lax
from jax.experimental import pallas as pl
from jax.experimental.pallas import tpu as pltpu
from jax.sharding import PartitionSpec as P

NZ = 64
STEPS = 4
BX = 4
BY = 4
COURANT = 0.55
MESH = pl.DeviceIdType.MESH


def split3(v):
    hi = v.astype(jnp.bfloat16)
    rest = v - hi.astype(jnp.float32)
    mid = rest.astype(jnp.bfloat16)
    low = (rest - mid.astype(jnp.float32)).astype(jnp.bfloat16)
    return jnp.concatenate([hi, mid, low], axis=0)


def kernel(
    n_gx, n_gy, cap,
    fwd, adj, perm, wave, cell, owner, slot, rows, out,
    E, H, fac, inc, asv, D, SE, SH, GE, GH, B, RB, S2, R2, RF, OH1, OH2,
    load_sem, perm_sem,
    exs, exr, hxs, hxr, eys, eyr, hys, hyr, src_sem, rt_s, rt_r,
):
    T = fac.shape[0]
    X = fac.shape[1]
    NS = fwd.shape[0]
    NB = out.shape[0]
    sims = 2 * NS
    src = lax.axis_index("src")
    gx = lax.axis_index("gx")
    gy = lax.axis_index("gy")

    loads = {}
    for sim in range(sims):
        state = fwd if sim < NS else adj
        s = sim % NS
        for xt in range(X // 8):
            loads[sim, 0, xt] = pltpu.make_async_copy(
                state.at[s, pl.ds(0, 3), xt],
                E.at[sim, :, pl.ds(0, T), pl.ds(8 * xt, 8), :],
                load_sem.at[sim, 0, xt],
            )
            loads[sim, 1, xt] = pltpu.make_async_copy(
                state.at[s, pl.ds(3, 3), xt],
                H.at[sim, :, pl.ds(1, T), pl.ds(8 + 8 * xt, 8), :],
                load_sem.at[sim, 1, xt],
            )
    perms = [
        pltpu.make_async_copy(
            perm.at[xt], fac.at[:, pl.ds(8 * xt, 8), :], perm_sem.at[xt]
        )
        for xt in range(X // 8)
    ]
    for sim in range(sims):
        for xt in range(X // 8):
            loads[sim, 0, xt].start()
    for sim in range(sims):
        for xt in range(X // 8):
            loads[sim, 1, xt].start()
    for c in perms:
        c.start()

    zero_tile = jnp.zeros((X, 128), jnp.float32)
    zero_row = jnp.zeros((1, 128), jnp.float32)
    for sim in range(sims):
        for c in (0, 2):
            E[sim, c, T, 0:X, :] = zero_tile
            H[sim, c, 0, 8 : 8 + X, :] = zero_tile

    def zero_ghosts(t, carry):
        for sim in range(sims):
            for c in (1, 2):
                E[sim, c, t, X : X + 1, :] = zero_row
                H[sim, c, t + 1, 7:8, :] = zero_row
        return carry

    lax.fori_loop(0, T, zero_ghosts, 0)

    barrier = pltpu.get_barrier_semaphore()
    partners = [
        {"gx": lax.rem(gx + 1, n_gx)},
        {"gx": lax.rem(gx + n_gx - 1, n_gx)},
        {"src": 1 - src},
    ]
    for d in range(1, n_gy):
        partners.append({"gy": lax.rem(gy + d, n_gy)})
    for device in partners:
        pl.semaphore_signal(barrier, inc=1, device_id=device, device_id_type=MESH)

    KB = 3 * NB
    LBY = owner.shape[1]
    dest = jnp.where(owner[...] >= 0, owner[...] * cap + slot[...], -1)
    dest = dest.astype(jnp.float32)
    q_i = lax.broadcasted_iota(jnp.int32, (LBY, KB), 0)
    b_i = lax.broadcasted_iota(jnp.int32, (LBY, KB), 1)
    pick = jnp.where(b_i % LBY == q_i, 1.0, 0.0)
    wide = jnp.dot(dest, pick, preferred_element_type=jnp.float32)
    p_i = lax.broadcasted_iota(jnp.int32, wide.shape, 0)
    l_i = lax.broadcasted_iota(jnp.int32, wide.shape, 1)
    line = jnp.sum(
        jnp.where((l_i % NB) // LBY == p_i, wide, 0.0), axis=0, keepdims=True
    )
    r_f = lax.broadcasted_iota(jnp.int32, (NB, KB), 0).astype(jnp.float32)
    OH1[...] = jnp.where(line == r_f, 1.0, 0.0).astype(jnp.bfloat16)
    m_i = lax.broadcasted_iota(jnp.int32, (NB, KB), 0)
    k_i = lax.broadcasted_iota(jnp.int32, (NB, KB), 1)
    pick = jnp.where(k_i % NB == m_i, 1.0, 0.0)
    row8 = jnp.broadcast_to(rows[...].astype(jnp.float32), (8, NB))
    line = jnp.dot(row8, pick, preferred_element_type=jnp.float32)[0:1, :]
    OH2[...] = jnp.where(line == r_f, 1.0, 0.0).astype(jnp.bfloat16)

    def e_copies(sim):
        x = pltpu.make_async_remote_copy(
            SE.at[sim], GE.at[sim], exs.at[sim], exr.at[sim],
            device_id={"gx": gx - 1}, device_id_type=MESH,
        )
        ys = [
            pltpu.make_async_remote_copy(
                E.at[sim, c, 0, pl.ds(0, X), :],
                E.at[sim, c, T, pl.ds(0, X), :],
                eys.at[sim, i], eyr.at[sim, i],
                device_id={"gy": gy - 1}, device_id_type=MESH,
            )
            for i, c in enumerate((0, 2))
        ]
        return x, ys

    def h_copies(sim):
        x = pltpu.make_async_remote_copy(
            SH.at[sim], GH.at[sim], hxs.at[sim], hxr.at[sim],
            device_id={"gx": gx + 1}, device_id_type=MESH,
        )
        ys = [
            pltpu.make_async_remote_copy(
                H.at[sim, c, T, pl.ds(8, X), :],
                H.at[sim, c, 0, pl.ds(8, X), :],
                hys.at[sim, i], hyr.at[sim, i],
                device_id={"gy": gy + 1}, device_id_type=MESH,
            )
            for i, c in enumerate((0, 2))
        ]
        return x, ys

    def e_send(sim):
        x, ys = e_copies(sim)

        @pl.when(gx > 0)
        def _():
            x.start()

        @pl.when(gy > 0)
        def _():
            for y in ys:
                y.start()

    def e_sent(sim):
        x, ys = e_copies(sim)

        @pl.when(gx > 0)
        def _():
            x.wait_send()

        @pl.when(gy > 0)
        def _():
            for y in ys:
                y.wait_send()

    def h_send(sim):
        x, ys = h_copies(sim)

        @pl.when(gx < n_gx - 1)
        def _():
            x.start()

        @pl.when(gy < n_gy - 1)
        def _():
            for y in ys:
                y.start()

    def h_sent(sim):
        x, ys = h_copies(sim)

        @pl.when(gx < n_gx - 1)
        def _():
            x.wait_send()

        @pl.when(gy < n_gy - 1)
        def _():
            for y in ys:
                y.wait_send()

    def e_arrive(sim):
        x, ys = e_copies(sim)

        @pl.when(gx < n_gx - 1)
        def _():
            x.wait_recv()

            def unpack(t, carry):
                E[sim, 1, t, X : X + 1, :] = GE[sim, 0, t]
                E[sim, 2, t, X : X + 1, :] = GE[sim, 1, t]
                return carry

            lax.fori_loop(0, T, unpack, 0, unroll=8)

        @pl.when(gy < n_gy - 1)
        def _():
            for y in ys:
                y.wait_recv()

    def h_arrive(sim):
        x, ys = h_copies(sim)

        @pl.when(gx > 0)
        def _():
            x.wait_recv()

            def unpack(t, carry):
                H[sim, 1, t + 1, 7:8, :] = GH[sim, 0, t]
                H[sim, 2, t + 1, 7:8, :] = GH[sim, 1, t]
                return carry

            lax.fori_loop(0, T, unpack, 0, unroll=8)

        @pl.when(gy > 0)
        def _():
            for y in ys:
                y.wait_recv()

    lane = lax.broadcasted_iota(jnp.int32, (X, 128), 1)
    row = lax.broadcasted_iota(jnp.int32, (X, 128), 0)
    z = lane % NZ
    z_first = z == 0
    z_last = z == NZ - 1
    low = lane < NZ
    cells_yz = T * 128
    linear = row * cells_yz + lane

    def h_phase(sim):
        def tile(t):
            ex = E[sim, 0, t, 0:X, :]
            ey = E[sim, 1, t, 0:X, :]
            ez = E[sim, 2, t, 0:X, :]
            exn = E[sim, 0, t + 1, 0:X, :]
            ezn = E[sim, 2, t + 1, 0:X, :]
            eyx = E[sim, 1, t, 1 : X + 1, :]
            ezx = E[sim, 2, t, 1 : X + 1, :]
            exy = pltpu.roll(jnp.where(low, exn, ex), NZ, 1)
            ezy = pltpu.roll(jnp.where(low, ezn, ez), NZ, 1)
            exz = jnp.where(z_last, 0.0, pltpu.roll(ex, 127, 1))
            eyz = jnp.where(z_last, 0.0, pltpu.roll(ey, 127, 1))
            hx = H[sim, 0, t + 1, 8 : 8 + X, :]
            hy = H[sim, 1, t + 1, 8 : 8 + X, :]
            hz = H[sim, 2, t + 1, 8 : 8 + X, :]
            hx = hx - COURANT * ((ezy - ez) - (eyz - ey))
            hy = hy - COURANT * ((exz - ex) - (ezx - ez))
            hz = hz - COURANT * ((eyx - ey) - (exy - ex))
            H[sim, 0, t + 1, 8 : 8 + X, :] = hx
            H[sim, 1, t + 1, 8 : 8 + X, :] = hy
            H[sim, 2, t + 1, 8 : 8 + X, :] = hz
            SH[sim, 0, t] = hy[X - 1 : X, :]
            SH[sim, 1, t] = hz[X - 1 : X, :]

        def body(i, carry):
            tile(2 * i)
            tile(2 * i + 1)
            return carry

        lax.fori_loop(0, T // 2, body, 0)

    def e_phase(sim, step):
        s = sim % NS
        forward = sim < NS
        if forward:
            lx = cell[s, 0] - gx * X
            lyz = (cell[s, 1] - gy * (cells_yz // NZ)) * NZ + cell[s, 2]
            inside = (lx >= 0) & (lx < X) & (lyz >= 0) & (lyz < cells_yz)
            target = jnp.where(inside, lx * cells_yz + lyz, -1)
            pulse = wave[s, step]

        def tile(t):
            hx = H[sim, 0, t + 1, 8 : 8 + X, :]
            hy = H[sim, 1, t + 1, 8 : 8 + X, :]
            hz = H[sim, 2, t + 1, 8 : 8 + X, :]
            hxp = H[sim, 0, t, 8 : 8 + X, :]
            hzp = H[sim, 2, t, 8 : 8 + X, :]
            hyx = H[sim, 1, t + 1, 7 : 7 + X, :]
            hzx = H[sim, 2, t + 1, 7 : 7 + X, :]
            hxy = pltpu.roll(jnp.where(low, hx, hxp), NZ, 1)
            hzy = pltpu.roll(jnp.where(low, hz, hzp), NZ, 1)
            hxz = jnp.where(z_first, 0.0, pltpu.roll(hx, 1, 1))
            hyz = jnp.where(z_first, 0.0, pltpu.roll(hy, 1, 1))
            f = fac[t]
            d0 = f * ((hz - hzy) - (hy - hyz))
            d1 = f * ((hx - hxz) - (hz - hzx))
            d2 = f * ((hy - hyx) - (hx - hxy))
            if forward:
                hit = linear == target - t * 128
                d2 = d2 + jnp.where(hit, pulse, 0.0)
            if not (forward and step == STEPS - 1):
                e0 = E[sim, 0, t, 0:X, :] + d0
                e1 = E[sim, 1, t, 0:X, :] + d1
                e2 = E[sim, 2, t, 0:X, :] + d2
            if step < STEPS - 1:
                E[sim, 0, t, 0:X, :] = e0
                E[sim, 1, t, 0:X, :] = e1
                E[sim, 2, t, 0:X, :] = e2
                SE[sim, 0, t] = e1[0:1, :]
                SE[sim, 1, t] = e2[0:1, :]
            if forward:
                if step < 2:
                    inc[s, step, 0, t] = d0
                    inc[s, step, 1, t] = d1
                    inc[s, step, 2, t] = d2
                else:
                    if step == 2:
                        a = [E[NS + s, c, t, 0:X, :] for c in range(3)]
                    else:
                        a = [asv[s, c, t] for c in range(3)]
                    term = d0 * a[0] + d1 * a[1] + d2 * a[2]
                    if step == 2 and s == 0:
                        D[t] = term
                    else:
                        D[t] = D[t] + term
            else:
                if step == 0:
                    asv[s, 0, t] = e0
                    asv[s, 1, t] = e1
                    asv[s, 2, t] = e2
                elif step >= 2:
                    k = STEPS - 1 - step
                    total = D[t] + (
                        e0 * inc[s, k, 0, t] + e1 * inc[s, k, 1, t] + e2 * inc[s, k, 2, t]
                    )
                    if step == STEPS - 1 and s == NS - 1:
                        total = total * (f * (-1.0 / COURANT))
                    D[t] = total

        def body(i, carry):
            tile(2 * i)
            tile(2 * i + 1)
            return carry

        lax.fori_loop(0, T // 2, body, 0)

    pl.semaphore_wait(barrier, len(partners))
    for sim in range(sims):
        for xt in range(X // 8):
            loads[sim, 0, xt].wait()

        def pack(t, carry):
            SE[sim, 0, t] = E[sim, 1, t, 0:1, :]
            SE[sim, 1, t] = E[sim, 2, t, 0:1, :]
            return carry

        lax.fori_loop(0, T, pack, 0, unroll=8)
        e_send(sim)

    for c in perms:
        c.wait()

    def make_factor(t, carry):
        fac[t] = COURANT / fac[t]
        return carry

    lax.fori_loop(0, T, make_factor, 0)

    for step in range(STEPS):
        for sim in range(sims):
            if step == 0:
                for xt in range(X // 8):
                    loads[sim, 1, xt].wait()
            e_arrive(sim)
            if step > 0:
                h_sent(sim)
            h_phase(sim)
            h_send(sim)
        for sim in range(sims):
            h_arrive(sim)
            e_sent(sim)
            e_phase(sim, step)
            if step < STEPS - 1:
                e_send(sim)
    for sim in range(sims):
        h_sent(sim)

    half = BX // 2
    for h in range(2):
        for p in range(X // BX):
            for xi in range(half):
                for yh in range(BY // 2):
                    j = xi * (BY // 2) + yh
                    start = yh * X + BX * p + half * h + xi
                    B[h, p * LBY : (p + 1) * LBY, j * 128 : (j + 1) * 128] = D.reshape(
                        T * X, 128
                    )[pl.ds(start, LBY, stride=2 * X), :]
    peer = pltpu.make_async_remote_copy(
        B.at[1 - src], RB, src_sem.at[0], src_sem.at[1],
        device_id={"src": 1 - src}, device_id_type=MESH,
    )
    peer.start()
    peer.wait_recv()
    mine = B[src] + RB[...]
    routed = jnp.dot(OH1[...], split3(mine), preferred_element_type=jnp.float32)
    for o in range(n_gy):
        S2[o] = routed[o * cap : (o + 1) * cap, :]
    sends = []
    for d in range(1, n_gy):
        o = lax.rem(gy + d, n_gy)
        sends.append(
            pltpu.make_async_remote_copy(
                S2.at[o], R2.at[gy], rt_s.at[d], rt_r.at[d],
                device_id={"gy": o}, device_id_type=MESH,
            )
        )
        sends[-1].start()
    R2[gy] = S2[gy]
    for c in sends:
        c.wait_recv()
    for o in range(n_gy):
        RF[o * cap : (o + 1) * cap, :] = R2[o]
    out[...] = jnp.dot(OH2[...], split3(RF[...]), preferred_element_type=jnp.float32)
    for c in sends:
        c.wait_send()
    peer.wait_send()


def tiled(state):
    lead = state.shape[:-2]
    x, yz = state.shape[-2:]
    n = len(lead)
    state = state.reshape(lead + (x // 8, 8, yz // 128, 128))
    return state.transpose(tuple(range(n)) + (n, n + 2, n + 1, n + 3))


def per_device(
    n_gx, n_gy, forward_state, adjoint_state, permittivity, waveform, source_cell,
    block_owner, block_slot, owner_rows,
):
    NS = forward_state.shape[0]
    X, YZ = permittivity.shape
    T = YZ // 128
    NB = block_owner.shape[0] * block_owner.shape[1]
    cap = max(2, (NB + n_gy - 1) // n_gy)
    cols = BX * BY * NZ // 2
    sims = 2 * NS
    f32 = jnp.float32
    dma = pltpu.SemaphoreType.DMA
    any_spec = pl.BlockSpec(memory_space=pl.ANY)
    vmem = pl.BlockSpec(memory_space=pltpu.VMEM)
    smem = pl.BlockSpec(memory_space=pltpu.SMEM)
    return pl.pallas_call(
        functools.partial(kernel, n_gx, n_gy, cap),
        out_shape=jax.ShapeDtypeStruct((NB, cols), f32),
        in_specs=[any_spec, any_spec, any_spec, smem, smem, vmem, vmem, vmem],
        out_specs=vmem,
        scratch_shapes=[
            pltpu.VMEM((sims, 3, T + 1, X + 8, 128), f32),
            pltpu.VMEM((sims, 3, T + 1, X + 8, 128), f32),
            pltpu.VMEM((T, X, 128), f32),
            pltpu.VMEM((NS, 2, 3, T, X, 128), f32),
            pltpu.VMEM((NS, 3, T, X, 128), f32),
            pltpu.VMEM((T, X, 128), f32),
            pltpu.VMEM((sims, 2, T, 1, 128), f32),
            pltpu.VMEM((sims, 2, T, 1, 128), f32),
            pltpu.VMEM((sims, 2, T, 1, 128), f32),
            pltpu.VMEM((sims, 2, T, 1, 128), f32),
            pltpu.VMEM((2, NB, cols), f32),
            pltpu.VMEM((NB, cols), f32),
            pltpu.VMEM((n_gy, cap, cols), f32),
            pltpu.VMEM((n_gy, cap, cols), f32),
            pltpu.VMEM((n_gy * cap, cols), f32),
            pltpu.VMEM((NB, 3 * NB), jnp.bfloat16),
            pltpu.VMEM((NB, 3 * NB), jnp.bfloat16),
            dma((sims, 2, X // 8)),
            dma((X // 8,)),
            dma((sims,)),
            dma((sims,)),
            dma((sims,)),
            dma((sims,)),
            dma((sims, 2)),
            dma((sims, 2)),
            dma((sims, 2)),
            dma((sims, 2)),
            dma((2,)),
            dma((n_gy,)),
            dma((n_gy,)),
        ],
        compiler_params=pltpu.CompilerParams(
            collective_id=0, has_side_effects=True, vmem_limit_bytes=48 * 1024 * 1024
        ),
    )(
        tiled(forward_state), tiled(adjoint_state), tiled(permittivity),
        waveform, source_cell, block_owner, block_slot, owner_rows,
    )


def solution(mesh):
    in_specs = (
        P("src", None, "gx", "gy"),
        P("src", None, "gx", "gy"),
        P("gx", "gy"),
        P("src", None),
        P("src", None),
        P("gx", "gy"),
        P("gx", "gy"),
        P(("gx", "gy"), None),
    )
    out_specs = P(("gx", "gy"), "src")
    sizes = dict(mesh.shape)
    return jax.shard_map(
        functools.partial(per_device, sizes["gx"], sizes["gy"]),
        mesh=mesh, in_specs=in_specs, out_specs=out_specs, check_vma=False,
    )
```

```python
import functools

import jax
import jax.numpy as jnp
from jax import lax
from jax.experimental import pallas as pl
from jax.experimental.pallas import tpu as pltpu
from jax.sharding import PartitionSpec as P

NZ = 64
STEPS = 4
BX = 4
BY = 4
UNROLL = 8
COURANT = 0.55
MESH = pl.DeviceIdType.MESH


def split3(v):
    hi = v.astype(jnp.bfloat16)
    rest = v - hi.astype(jnp.float32)
    mid = rest.astype(jnp.bfloat16)
    low = (rest - mid.astype(jnp.float32)).astype(jnp.bfloat16)
    return jnp.concatenate([hi, mid, low], axis=0)


def kernel(
    n_gx, n_gy, cap,
    fwd, adj, perm, wave_hbm, cell_hbm, owner_hbm, slot_hbm, rows_hbm, out,
    E, H, fac, inc, asv, D, SE, SH, GE, GH, B, RB, S2, R2, RF, OH1, OH2,
    wave, cell, owner, slot, rows, small_sem,
    load_sem, perm_sem,
    exs, exr, hxs, hxr, eys, eyr, hys, hyr, src_sem, rt_s, rt_r,
):
    T = fac.shape[0]
    X = fac.shape[1]
    NS = fwd.shape[0]
    NB = out.shape[0]
    sims = 2 * NS
    src = lax.axis_index("src")
    gx = lax.axis_index("gx")
    gy = lax.axis_index("gy")

    loads = {}
    for sim in range(sims):
        state = fwd if sim < NS else adj
        s = sim % NS
        for xt in range(X // 8):
            loads[sim, 0, xt] = pltpu.make_async_copy(
                state.at[s, pl.ds(0, 3), xt],
                E.at[sim, :, pl.ds(0, T), pl.ds(8 * xt, 8), :],
                load_sem.at[sim, 0, xt],
            )
            loads[sim, 1, xt] = pltpu.make_async_copy(
                state.at[s, pl.ds(3, 3), xt],
                H.at[sim, :, pl.ds(1, T), pl.ds(8 + 8 * xt, 8), :],
                load_sem.at[sim, 1, xt],
            )
    perms = [
        pltpu.make_async_copy(
            perm.at[xt], fac.at[:, pl.ds(8 * xt, 8), :], perm_sem.at[xt]
        )
        for xt in range(X // 8)
    ]
    for sim in range(sims):
        for xt in range(X // 8):
            loads[sim, 0, xt].start()
    for sim in range(sims):
        for xt in range(X // 8):
            loads[sim, 1, xt].start()
    smalls = [
        pltpu.make_async_copy(a, b, small_sem.at[i])
        for i, (a, b) in enumerate(
            (
                (wave_hbm, wave), (cell_hbm, cell), (owner_hbm, owner),
                (slot_hbm, slot), (rows_hbm, rows),
            )
        )
    ]
    for c in smalls:
        c.start()
    for c in perms:
        c.start()

    zero_tile = jnp.zeros((X, 128), jnp.float32)
    zero_row = jnp.zeros((1, 128), jnp.float32)
    for sim in range(sims):
        for c in (0, 2):
            E[sim, c, T, 0:X, :] = zero_tile
            H[sim, c, 0, 8 : 8 + X, :] = zero_tile

    def zero_ghosts(t, carry):
        for sim in range(sims):
            for c in (1, 2):
                E[sim, c, t, X : X + 1, :] = zero_row
                H[sim, c, t + 1, 7:8, :] = zero_row
        return carry

    lax.fori_loop(0, T, zero_ghosts, 0, unroll=4)

    barrier = pltpu.get_barrier_semaphore()
    partners = [
        {"gx": lax.rem(gx + 1, n_gx)},
        {"gx": lax.rem(gx + n_gx - 1, n_gx)},
        {"src": 1 - src},
    ]
    for d in range(1, n_gy):
        partners.append({"gy": lax.rem(gy + d, n_gy)})
    for device in partners:
        pl.semaphore_signal(barrier, inc=1, device_id=device, device_id_type=MESH)

    for c in smalls:
        c.wait()
    KB = 3 * NB
    LBY = owner.shape[1]
    dest = jnp.where(owner[...] >= 0, owner[...] * cap + slot[...], -1)
    dest = dest.astype(jnp.float32)
    q_i = lax.broadcasted_iota(jnp.int32, (LBY, KB), 0)
    b_i = lax.broadcasted_iota(jnp.int32, (LBY, KB), 1)
    pick = jnp.where(b_i % LBY == q_i, 1.0, 0.0)
    wide = jnp.dot(dest, pick, preferred_element_type=jnp.float32)
    p_i = lax.broadcasted_iota(jnp.int32, wide.shape, 0)
    l_i = lax.broadcasted_iota(jnp.int32, wide.shape, 1)
    line = jnp.sum(
        jnp.where((l_i % NB) // LBY == p_i, wide, 0.0), axis=0, keepdims=True
    )
    r_f = lax.broadcasted_iota(jnp.int32, (NB, KB), 0).astype(jnp.float32)
    OH1[...] = jnp.where(line == r_f, 1.0, 0.0).astype(jnp.bfloat16)
    m_i = lax.broadcasted_iota(jnp.int32, (NB, KB), 0)
    k_i = lax.broadcasted_iota(jnp.int32, (NB, KB), 1)
    pick = jnp.where(k_i % NB == m_i, 1.0, 0.0)
    row8 = jnp.broadcast_to(rows[...].astype(jnp.float32), (8, NB))
    line = jnp.dot(row8, pick, preferred_element_type=jnp.float32)[0:1, :]
    OH2[...] = jnp.where(line == r_f, 1.0, 0.0).astype(jnp.bfloat16)

    def e_copies(sim):
        x = pltpu.make_async_remote_copy(
            SE.at[sim], GE.at[sim], exs.at[sim], exr.at[sim],
            device_id={"gx": gx - 1}, device_id_type=MESH,
        )
        ys = [
            pltpu.make_async_remote_copy(
                E.at[sim, c, 0, pl.ds(0, X), :],
                E.at[sim, c, T, pl.ds(0, X), :],
                eys.at[sim, i], eyr.at[sim, i],
                device_id={"gy": gy - 1}, device_id_type=MESH,
            )
            for i, c in enumerate((0, 2))
        ]
        return x, ys

    def h_copies(sim):
        x = pltpu.make_async_remote_copy(
            SH.at[sim], GH.at[sim], hxs.at[sim], hxr.at[sim],
            device_id={"gx": gx + 1}, device_id_type=MESH,
        )
        ys = [
            pltpu.make_async_remote_copy(
                H.at[sim, c, T, pl.ds(8, X), :],
                H.at[sim, c, 0, pl.ds(8, X), :],
                hys.at[sim, i], hyr.at[sim, i],
                device_id={"gy": gy + 1}, device_id_type=MESH,
            )
            for i, c in enumerate((0, 2))
        ]
        return x, ys

    def e_send(sim):
        x, ys = e_copies(sim)

        @pl.when(gx > 0)
        def _():
            x.start()

        @pl.when(gy > 0)
        def _():
            for y in ys:
                y.start()

    def e_sent(sim):
        x, ys = e_copies(sim)

        @pl.when(gx > 0)
        def _():
            x.wait_send()

        @pl.when(gy > 0)
        def _():
            for y in ys:
                y.wait_send()

    def h_send(sim):
        x, ys = h_copies(sim)

        @pl.when(gx < n_gx - 1)
        def _():
            x.start()

        @pl.when(gy < n_gy - 1)
        def _():
            for y in ys:
                y.start()

    def h_sent(sim):
        x, ys = h_copies(sim)

        @pl.when(gx < n_gx - 1)
        def _():
            x.wait_send()

        @pl.when(gy < n_gy - 1)
        def _():
            for y in ys:
                y.wait_send()

    def e_arrive(sim):
        x, ys = e_copies(sim)

        @pl.when(gx < n_gx - 1)
        def _():
            x.wait_recv()

            def unpack(t, carry):
                E[sim, 1, t, X : X + 1, :] = GE[sim, 0, t]
                E[sim, 2, t, X : X + 1, :] = GE[sim, 1, t]
                return carry

            lax.fori_loop(0, T, unpack, 0, unroll=True)

        @pl.when(gy < n_gy - 1)
        def _():
            for y in ys:
                y.wait_recv()

    def h_arrive(sim):
        x, ys = h_copies(sim)

        @pl.when(gx > 0)
        def _():
            x.wait_recv()

            def unpack(t, carry):
                H[sim, 1, t + 1, 7:8, :] = GH[sim, 0, t]
                H[sim, 2, t + 1, 7:8, :] = GH[sim, 1, t]
                return carry

            lax.fori_loop(0, T, unpack, 0, unroll=True)

        @pl.when(gy > 0)
        def _():
            for y in ys:
                y.wait_recv()

    lane = lax.broadcasted_iota(jnp.int32, (X, 128), 1)
    row = lax.broadcasted_iota(jnp.int32, (X, 128), 0)
    z = lane % NZ
    z_first = z == 0
    z_last = z == NZ - 1
    low = lane < NZ
    cells_yz = T * 128
    linear = row * cells_yz + lane

    def h_phase(sim, step):
        def tile(t):
            ex = E[sim, 0, t, 0:X, :]
            ey = E[sim, 1, t, 0:X, :]
            ez = E[sim, 2, t, 0:X, :]
            exn = E[sim, 0, t + 1, 0:X, :]
            ezn = E[sim, 2, t + 1, 0:X, :]
            eyx = E[sim, 1, t, 1 : X + 1, :]
            ezx = E[sim, 2, t, 1 : X + 1, :]
            exy = pltpu.roll(jnp.where(low, exn, ex), NZ, 1)
            ezy = pltpu.roll(jnp.where(low, ezn, ez), NZ, 1)
            exz = jnp.where(z_last, 0.0, pltpu.roll(ex, 127, 1))
            eyz = jnp.where(z_last, 0.0, pltpu.roll(ey, 127, 1))
            hx = H[sim, 0, t + 1, 8 : 8 + X, :]
            hy = H[sim, 1, t + 1, 8 : 8 + X, :]
            hz = H[sim, 2, t + 1, 8 : 8 + X, :]
            if step == 0:
                hx = hx * (1.0 / COURANT)
                hy = hy * (1.0 / COURANT)
                hz = hz * (1.0 / COURANT)
            hx = hx - ((ezy - ez) - (eyz - ey))
            hy = hy - ((exz - ex) - (ezx - ez))
            hz = hz - ((eyx - ey) - (exy - ex))
            H[sim, 0, t + 1, 8 : 8 + X, :] = hx
            H[sim, 1, t + 1, 8 : 8 + X, :] = hy
            H[sim, 2, t + 1, 8 : 8 + X, :] = hz
            SH[sim, 0, t] = hy[X - 1 : X, :]
            SH[sim, 1, t] = hz[X - 1 : X, :]

        def body(i, carry):
            for k in range(UNROLL):
                tile(UNROLL * i + k)
            return carry

        lax.fori_loop(0, T // UNROLL, body, 0)

    def e_phase(sim, step):
        s = sim % NS
        forward = sim < NS
        if forward:
            lx = cell[s, 0] - gx * X
            lyz = (cell[s, 1] - gy * (cells_yz // NZ)) * NZ + cell[s, 2]
            inside = (lx >= 0) & (lx < X) & (lyz >= 0) & (lyz < cells_yz)
            target = jnp.where(inside, lx * cells_yz + lyz, -1)
            pulse = wave[s, step]

        def tile(t):
            hx = H[sim, 0, t + 1, 8 : 8 + X, :]
            hy = H[sim, 1, t + 1, 8 : 8 + X, :]
            hz = H[sim, 2, t + 1, 8 : 8 + X, :]
            hxp = H[sim, 0, t, 8 : 8 + X, :]
            hzp = H[sim, 2, t, 8 : 8 + X, :]
            hyx = H[sim, 1, t + 1, 7 : 7 + X, :]
            hzx = H[sim, 2, t + 1, 7 : 7 + X, :]
            hxy = pltpu.roll(jnp.where(low, hx, hxp), NZ, 1)
            hzy = pltpu.roll(jnp.where(low, hz, hzp), NZ, 1)
            hxz = jnp.where(z_first, 0.0, pltpu.roll(hx, 1, 1))
            hyz = jnp.where(z_first, 0.0, pltpu.roll(hy, 1, 1))
            f = fac[t]
            d0 = f * ((hz - hzy) - (hy - hyz))
            d1 = f * ((hx - hxz) - (hz - hzx))
            d2 = f * ((hy - hyx) - (hx - hxy))
            if forward:
                hit = linear == target - t * 128
                d2 = d2 + jnp.where(hit, pulse, 0.0)
            if not (forward and step == STEPS - 1):
                e0 = E[sim, 0, t, 0:X, :] + d0
                e1 = E[sim, 1, t, 0:X, :] + d1
                e2 = E[sim, 2, t, 0:X, :] + d2
            if step < STEPS - 1:
                E[sim, 0, t, 0:X, :] = e0
                E[sim, 1, t, 0:X, :] = e1
                E[sim, 2, t, 0:X, :] = e2
                SE[sim, 0, t] = e1[0:1, :]
                SE[sim, 1, t] = e2[0:1, :]
            if forward:
                if step < 2:
                    inc[s, step, 0, t] = d0
                    inc[s, step, 1, t] = d1
                    inc[s, step, 2, t] = d2
                else:
                    if step == 2:
                        a = [E[NS + s, c, t, 0:X, :] for c in range(3)]
                    else:
                        a = [asv[s, c, t] for c in range(3)]
                    term = d0 * a[0] + d1 * a[1] + d2 * a[2]
                    if step == 2 and s == 0:
                        D[t] = term
                    else:
                        D[t] = D[t] + term
            else:
                if step == 0:
                    asv[s, 0, t] = e0
                    asv[s, 1, t] = e1
                    asv[s, 2, t] = e2
                elif step >= 2:
                    k = STEPS - 1 - step
                    total = D[t] + (
                        e0 * inc[s, k, 0, t] + e1 * inc[s, k, 1, t] + e2 * inc[s, k, 2, t]
                    )
                    if step == STEPS - 1 and s == NS - 1:
                        total = total * (f * (-1.0 / (COURANT * COURANT)))
                    D[t] = total

        def body(i, carry):
            for k in range(UNROLL):
                tile(UNROLL * i + k)
            return carry

        lax.fori_loop(0, T // UNROLL, body, 0)

    pl.semaphore_wait(barrier, len(partners))
    for sim in range(sims):
        for xt in range(X // 8):
            loads[sim, 0, xt].wait()

        def pack(t, carry):
            SE[sim, 0, t] = E[sim, 1, t, 0:1, :]
            SE[sim, 1, t] = E[sim, 2, t, 0:1, :]
            return carry

        lax.fori_loop(0, T, pack, 0, unroll=True)
        e_send(sim)

    for c in perms:
        c.wait()

    def make_factor(t, carry):
        fac[t] = (COURANT * COURANT) / fac[t]
        return carry

    lax.fori_loop(0, T, make_factor, 0, unroll=8)

    for step in range(STEPS):
        for sim in range(sims):
            if step == 0:
                for xt in range(X // 8):
                    loads[sim, 1, xt].wait()
            e_arrive(sim)
            if step > 0:
                h_sent(sim)
            h_phase(sim, step)
            h_send(sim)
        for sim in range(sims):
            h_arrive(sim)
            e_sent(sim)
            e_phase(sim, step)
            if step < STEPS - 1:
                e_send(sim)
    for sim in range(sims):
        h_sent(sim)

    half = BX // 2
    for h in range(2):
        for p in range(X // BX):
            for xi in range(half):
                for yh in range(BY // 2):
                    j = xi * (BY // 2) + yh
                    start = yh * X + BX * p + half * h + xi
                    B[h, p * LBY : (p + 1) * LBY, j * 128 : (j + 1) * 128] = D.reshape(
                        T * X, 128
                    )[pl.ds(start, LBY, stride=2 * X), :]
    peer = pltpu.make_async_remote_copy(
        B.at[1 - src], RB, src_sem.at[0], src_sem.at[1],
        device_id={"src": 1 - src}, device_id_type=MESH,
    )
    peer.start()
    peer.wait_recv()
    mine = B[src] + RB[...]
    routed = jnp.dot(OH1[...], split3(mine), preferred_element_type=jnp.float32)
    for o in range(n_gy):
        S2[o] = routed[o * cap : (o + 1) * cap, :]
    sends = []
    for d in range(1, n_gy):
        o = lax.rem(gy + d, n_gy)
        sends.append(
            pltpu.make_async_remote_copy(
                S2.at[o], R2.at[gy], rt_s.at[d], rt_r.at[d],
                device_id={"gy": o}, device_id_type=MESH,
            )
        )
        sends[-1].start()
    R2[gy] = S2[gy]
    for c in sends:
        c.wait_recv()
    for o in range(n_gy):
        RF[o * cap : (o + 1) * cap, :] = R2[o]
    out[...] = jnp.dot(OH2[...], split3(RF[...]), preferred_element_type=jnp.float32)
    for c in sends:
        c.wait_send()
    peer.wait_send()


def tiled(state):
    lead = state.shape[:-2]
    x, yz = state.shape[-2:]
    n = len(lead)
    state = state.reshape(lead + (x // 8, 8, yz // 128, 128))
    return state.transpose(tuple(range(n)) + (n, n + 2, n + 1, n + 3))


def per_device(
    n_gx, n_gy, forward_state, adjoint_state, permittivity, waveform, source_cell,
    block_owner, block_slot, owner_rows,
):
    NS = forward_state.shape[0]
    X, YZ = permittivity.shape
    T = YZ // 128
    NB = block_owner.shape[0] * block_owner.shape[1]
    cap = max(2, (NB + n_gy - 1) // n_gy)
    cols = BX * BY * NZ // 2
    sims = 2 * NS
    f32 = jnp.float32
    dma = pltpu.SemaphoreType.DMA
    any_spec = pl.BlockSpec(memory_space=pl.ANY)
    vmem = pl.BlockSpec(memory_space=pltpu.VMEM)
    return pl.pallas_call(
        functools.partial(kernel, n_gx, n_gy, cap),
        out_shape=jax.ShapeDtypeStruct((NB, cols), f32),
        in_specs=[any_spec] * 8,
        out_specs=vmem,
        scratch_shapes=[
            pltpu.VMEM((sims, 3, T + 1, X + 8, 128), f32),
            pltpu.VMEM((sims, 3, T + 1, X + 8, 128), f32),
            pltpu.VMEM((T, X, 128), f32),
            pltpu.VMEM((NS, 2, 3, T, X, 128), f32),
            pltpu.VMEM((NS, 3, T, X, 128), f32),
            pltpu.VMEM((T, X, 128), f32),
            pltpu.VMEM((sims, 2, T, 1, 128), f32),
            pltpu.VMEM((sims, 2, T, 1, 128), f32),
            pltpu.VMEM((sims, 2, T, 1, 128), f32),
            pltpu.VMEM((sims, 2, T, 1, 128), f32),
            pltpu.VMEM((2, NB, cols), f32),
            pltpu.VMEM((NB, cols), f32),
            pltpu.VMEM((n_gy, cap, cols), f32),
            pltpu.VMEM((n_gy, cap, cols), f32),
            pltpu.VMEM((n_gy * cap, cols), f32),
            pltpu.VMEM((NB, 3 * NB), jnp.bfloat16),
            pltpu.VMEM((NB, 3 * NB), jnp.bfloat16),
            pltpu.SMEM(waveform.shape, f32),
            pltpu.SMEM(source_cell.shape, jnp.int32),
            pltpu.VMEM(block_owner.shape, jnp.int32),
            pltpu.VMEM(block_slot.shape, jnp.int32),
            pltpu.VMEM(owner_rows.shape, jnp.int32),
            dma((5,)),
            dma((sims, 2, X // 8)),
            dma((X // 8,)),
            dma((sims,)),
            dma((sims,)),
            dma((sims,)),
            dma((sims,)),
            dma((sims, 2)),
            dma((sims, 2)),
            dma((sims, 2)),
            dma((sims, 2)),
            dma((2,)),
            dma((n_gy,)),
            dma((n_gy,)),
        ],
        compiler_params=pltpu.CompilerParams(
            collective_id=0, has_side_effects=True, vmem_limit_bytes=62 * 1024 * 1024
        ),
    )(
        tiled(forward_state), tiled(adjoint_state), tiled(permittivity),
        waveform, source_cell, block_owner, block_slot, owner_rows,
    )


def solution(mesh):
    in_specs = (
        P("src", None, "gx", "gy"),
        P("src", None, "gx", "gy"),
        P("gx", "gy"),
        P("src", None),
        P("src", None),
        P("gx", "gy"),
        P("gx", "gy"),
        P(("gx", "gy"), None),
    )
    out_specs = P(("gx", "gy"), "src")
    sizes = dict(mesh.shape)
    return jax.shard_map(
        functools.partial(per_device, sizes["gx"], sizes["gy"]),
        mesh=mesh, in_specs=in_specs, out_specs=out_specs, check_vma=False,
    )
```

```python
import functools

import jax
import jax.numpy as jnp
from jax import lax
from jax.experimental import pallas as pl
from jax.experimental.pallas import tpu as pltpu
from jax.sharding import PartitionSpec as P

NZ = 64
STEPS = 4
BX = 4
BY = 4
UNROLL = 8
COURANT = 0.55
MESH = pl.DeviceIdType.MESH


def split3(v):
    hi = v.astype(jnp.bfloat16)
    rest = v - hi.astype(jnp.float32)
    mid = rest.astype(jnp.bfloat16)
    low = (rest - mid.astype(jnp.float32)).astype(jnp.bfloat16)
    return jnp.concatenate([hi, mid, low], axis=0)


def kernel(
    n_gx, n_gy, cap,
    fwd, adj, perm, wave_hbm, cell_hbm, owner_hbm, slot_hbm, rows_hbm, out,
    ST, PS, YE, YH, E, H, fac, inc, asv, D, SE, SH, GE, GH, B, RB, S2, R2, RF, OH1, OH2,
    wave, cell, owner, slot, rows, small_sem,
    load_sem, perm_sem,
    exs, exr, hxs, hxr, eys, eyr, hys, hyr, src_sem, rt_s, rt_r,
):
    T = fac.shape[0]
    X = fac.shape[1]
    NS = fwd.shape[0]
    NB = out.shape[0]
    sims = 2 * NS
    src = lax.axis_index("src")
    gx = lax.axis_index("gx")
    gy = lax.axis_index("gy")

    loads = {}
    for sim in range(sims):
        state = fwd if sim < NS else adj
        s = sim % NS
        for xt in range(X // 8):
            loads[sim, 0, xt] = pltpu.make_async_copy(
                state.at[s, pl.ds(0, 3), xt],
                ST.at[sim, pl.ds(0, 3), :, pl.ds(8 * xt, 8), :],
                load_sem.at[sim, 0, xt],
            )
            loads[sim, 1, xt] = pltpu.make_async_copy(
                state.at[s, pl.ds(3, 3), xt],
                ST.at[sim, pl.ds(3, 3), :, pl.ds(8 * xt, 8), :],
                load_sem.at[sim, 1, xt],
            )
    perms = [
        pltpu.make_async_copy(
            perm.at[xt], PS.at[:, pl.ds(8 * xt, 8), :], perm_sem.at[xt]
        )
        for xt in range(X // 8)
    ]
    for sim in range(sims):
        for xt in range(X // 8):
            loads[sim, 0, xt].start()
    for sim in range(sims):
        for xt in range(X // 8):
            loads[sim, 1, xt].start()
    smalls = [
        pltpu.make_async_copy(a, b, small_sem.at[i])
        for i, (a, b) in enumerate(
            (
                (wave_hbm, wave), (cell_hbm, cell), (owner_hbm, owner),
                (slot_hbm, slot), (rows_hbm, rows),
            )
        )
    ]
    for c in smalls:
        c.start()
    for c in perms:
        c.start()

    R = X + 8
    EF = E.reshape(sims * 3 * (T + 1) * R, 128)
    HF = H.reshape(sims * 3 * (T + 1) * R, 128)

    def e_row(sim, c, r):
        return pl.ds((sim * 3 + c) * (T + 1) * R + r, T, stride=R), slice(None)

    def h_row(sim, c, r):
        return e_row(sim, c, R + r)

    zero_tile = jnp.zeros((X, 128), jnp.float32)
    zero_rows = jnp.zeros((T, 128), jnp.float32)
    for sim in range(sims):
        for i in range(2):
            YE[sim, i] = zero_tile
            YH[sim, i] = zero_tile
            EF[e_row(sim, 1 + i, X)] = zero_rows
            HF[h_row(sim, 1 + i, 7)] = zero_rows

    barrier = pltpu.get_barrier_semaphore()
    partners = [
        {"gx": lax.rem(gx + 1, n_gx)},
        {"gx": lax.rem(gx + n_gx - 1, n_gx)},
        {"src": 1 - src},
    ]
    for d in range(1, n_gy):
        partners.append({"gy": lax.rem(gy + d, n_gy)})
    for device in partners:
        pl.semaphore_signal(barrier, inc=1, device_id=device, device_id_type=MESH)

    for c in smalls:
        c.wait()
    KB = 3 * NB
    LBY = owner.shape[1]
    dest = jnp.where(owner[...] >= 0, owner[...] * cap + slot[...], -1)
    dest = dest.astype(jnp.float32)
    q_i = lax.broadcasted_iota(jnp.int32, (LBY, KB), 0)
    b_i = lax.broadcasted_iota(jnp.int32, (LBY, KB), 1)
    pick = jnp.where(b_i % LBY == q_i, 1.0, 0.0)
    wide = jnp.dot(dest, pick, preferred_element_type=jnp.float32)
    p_i = lax.broadcasted_iota(jnp.int32, wide.shape, 0)
    l_i = lax.broadcasted_iota(jnp.int32, wide.shape, 1)
    line = jnp.sum(
        jnp.where((l_i % NB) // LBY == p_i, wide, 0.0), axis=0, keepdims=True
    )
    r_f = lax.broadcasted_iota(jnp.int32, (NB, KB), 0).astype(jnp.float32)
    OH1[...] = jnp.where(line == r_f, 1.0, 0.0).astype(jnp.bfloat16)
    m_i = lax.broadcasted_iota(jnp.int32, (NB, KB), 0)
    k_i = lax.broadcasted_iota(jnp.int32, (NB, KB), 1)
    pick = jnp.where(k_i % NB == m_i, 1.0, 0.0)
    row8 = jnp.broadcast_to(rows[...].astype(jnp.float32), (8, NB))
    line = jnp.dot(row8, pick, preferred_element_type=jnp.float32)[0:1, :]
    OH2[...] = jnp.where(line == r_f, 1.0, 0.0).astype(jnp.bfloat16)

    lane = lax.broadcasted_iota(jnp.int32, (X, 128), 1)
    row = lax.broadcasted_iota(jnp.int32, (X, 128), 0)
    z = lane % NZ
    z_first = z == 0
    z_last = z == NZ - 1
    low = lane < NZ
    cells_yz = T * 128
    linear = row * cells_yz + jnp.where(low, z, z + T * NZ)

    def e_copies(sim):
        x = pltpu.make_async_remote_copy(
            SE.at[sim], GE.at[sim], exs.at[sim], exr.at[sim],
            device_id={"gx": gx - 1}, device_id_type=MESH,
        )
        ys = [
            pltpu.make_async_remote_copy(
                E.at[sim, c, 0, pl.ds(0, X), :],
                YE.at[sim, i],
                eys.at[sim, i], eyr.at[sim, i],
                device_id={"gy": gy - 1}, device_id_type=MESH,
            )
            for i, c in enumerate((0, 2))
        ]
        return x, ys

    def h_copies(sim):
        x = pltpu.make_async_remote_copy(
            SH.at[sim], GH.at[sim], hxs.at[sim], hxr.at[sim],
            device_id={"gx": gx + 1}, device_id_type=MESH,
        )
        ys = [
            pltpu.make_async_remote_copy(
                H.at[sim, c, T, pl.ds(8, X), :],
                YH.at[sim, i],
                hys.at[sim, i], hyr.at[sim, i],
                device_id={"gy": gy + 1}, device_id_type=MESH,
            )
            for i, c in enumerate((0, 2))
        ]
        return x, ys

    def e_send(sim):
        x, ys = e_copies(sim)

        @pl.when(gx > 0)
        def _():
            x.start()

        @pl.when(gy > 0)
        def _():
            for y in ys:
                y.start()

    def e_sent(sim):
        x, ys = e_copies(sim)

        @pl.when(gx > 0)
        def _():
            x.wait_send()

        @pl.when(gy > 0)
        def _():
            for y in ys:
                y.wait_send()

    def h_send(sim):
        x, ys = h_copies(sim)

        @pl.when(gx < n_gx - 1)
        def _():
            x.start()

        @pl.when(gy < n_gy - 1)
        def _():
            for y in ys:
                y.start()

    def h_sent(sim):
        x, ys = h_copies(sim)

        @pl.when(gx < n_gx - 1)
        def _():
            x.wait_send()

        @pl.when(gy < n_gy - 1)
        def _():
            for y in ys:
                y.wait_send()

    def e_arrive(sim):
        x, ys = e_copies(sim)

        @pl.when(gx < n_gx - 1)
        def _():
            x.wait_recv()
            for i in range(2):
                EF[e_row(sim, 1 + i, X)] = GE[sim, i]

        @pl.when(gy < n_gy - 1)
        def _():
            for y in ys:
                y.wait_recv()

        for i, c in enumerate((0, 2)):
            edge = jnp.where(low, YE[sim, i], E[sim, c, 0, 0:X, :])
            E[sim, c, T, 0:X, :] = pltpu.roll(edge, NZ, 1)

    def h_arrive(sim):
        x, ys = h_copies(sim)

        @pl.when(gx > 0)
        def _():
            x.wait_recv()
            for i in range(2):
                HF[h_row(sim, 1 + i, 7)] = GH[sim, i]

        @pl.when(gy > 0)
        def _():
            for y in ys:
                y.wait_recv()

        for i, c in enumerate((0, 2)):
            edge = jnp.where(low, H[sim, c, T, 8 : 8 + X, :], YH[sim, i])
            H[sim, c, 0, 8 : 8 + X, :] = pltpu.roll(edge, NZ, 1)

    def h_phase(sim):
        def tile(t, held):
            ex, ez = held
            ey = E[sim, 1, t, 0:X, :]
            exn = E[sim, 0, t + 1, 0:X, :]
            ezn = E[sim, 2, t + 1, 0:X, :]
            eyx = E[sim, 1, t, 1 : X + 1, :]
            ezx = E[sim, 2, t, 1 : X + 1, :]
            exz = jnp.where(z_last, 0.0, pltpu.roll(ex, 127, 1))
            eyz = jnp.where(z_last, 0.0, pltpu.roll(ey, 127, 1))
            hx = H[sim, 0, t + 1, 8 : 8 + X, :]
            hy = H[sim, 1, t + 1, 8 : 8 + X, :]
            hz = H[sim, 2, t + 1, 8 : 8 + X, :]
            hx = hx - ((ezn - ez) - (eyz - ey))
            hy = hy - ((exz - ex) - (ezx - ez))
            hz = hz - ((eyx - ey) - (exn - ex))
            H[sim, 0, t + 1, 8 : 8 + X, :] = hx
            H[sim, 1, t + 1, 8 : 8 + X, :] = hy
            H[sim, 2, t + 1, 8 : 8 + X, :] = hz
            return exn, ezn

        def body(i, carry):
            held = (
                E[sim, 0, UNROLL * i, 0:X, :],
                E[sim, 2, UNROLL * i, 0:X, :],
            )
            for k in range(UNROLL):
                held = tile(UNROLL * i + k, held)
            return carry

        lax.fori_loop(0, T // UNROLL, body, 0)
        for i in range(2):
            SH[sim, i] = HF[h_row(sim, 1 + i, 7 + X)]

    def e_phase(sim, step):
        s = sim % NS
        forward = sim < NS
        if forward:
            lx = cell[s, 0] - gx * X
            lyz = (cell[s, 1] - gy * (cells_yz // NZ)) * NZ + cell[s, 2]
            inside = (lx >= 0) & (lx < X) & (lyz >= 0) & (lyz < cells_yz)
            target = jnp.where(inside, lx * cells_yz + lyz, -1)
            pulse = wave[s, step]

        def tile(t, held):
            hxp, hzp = held
            hx = H[sim, 0, t + 1, 8 : 8 + X, :]
            hy = H[sim, 1, t + 1, 8 : 8 + X, :]
            hz = H[sim, 2, t + 1, 8 : 8 + X, :]
            hyx = H[sim, 1, t + 1, 7 : 7 + X, :]
            hzx = H[sim, 2, t + 1, 7 : 7 + X, :]
            hxz = jnp.where(z_first, 0.0, pltpu.roll(hx, 1, 1))
            hyz = jnp.where(z_first, 0.0, pltpu.roll(hy, 1, 1))
            f = fac[t]
            d0 = f * ((hz - hzp) - (hy - hyz))
            d1 = f * ((hx - hxz) - (hz - hzx))
            d2 = f * ((hy - hyx) - (hx - hxp))
            if forward:
                hit = linear == target - t * NZ
                d2 = d2 + jnp.where(hit, pulse, 0.0)
            if not (forward and step == STEPS - 1):
                e0 = E[sim, 0, t, 0:X, :] + d0
                e1 = E[sim, 1, t, 0:X, :] + d1
                e2 = E[sim, 2, t, 0:X, :] + d2
            if step < STEPS - 1:
                E[sim, 0, t, 0:X, :] = e0
                E[sim, 1, t, 0:X, :] = e1
                E[sim, 2, t, 0:X, :] = e2
            if forward:
                if step < 2:
                    inc[s, step, 0, t] = d0
                    inc[s, step, 1, t] = d1
                    inc[s, step, 2, t] = d2
                else:
                    if step == 2:
                        a = [E[NS + s, c, t, 0:X, :] for c in range(3)]
                    else:
                        a = [asv[s, c, t] for c in range(3)]
                    term = d0 * a[0] + d1 * a[1] + d2 * a[2]
                    if step == 2 and s == 0:
                        D[t] = term
                    else:
                        D[t] = D[t] + term
            else:
                if step == 0:
                    asv[s, 0, t] = e0
                    asv[s, 1, t] = e1
                    asv[s, 2, t] = e2
                elif step >= 2:
                    k = STEPS - 1 - step
                    total = D[t] + (
                        e0 * inc[s, k, 0, t] + e1 * inc[s, k, 1, t] + e2 * inc[s, k, 2, t]
                    )
                    if step == STEPS - 1 and s == NS - 1:
                        total = total * (f * (-1.0 / (COURANT * COURANT)))
                    D[t] = total
            return hx, hz

        def body(i, carry):
            held = (
                H[sim, 0, UNROLL * i, 8 : 8 + X, :],
                H[sim, 2, UNROLL * i, 8 : 8 + X, :],
            )
            for k in range(UNROLL):
                held = tile(UNROLL * i + k, held)
            return carry

        lax.fori_loop(0, T // UNROLL, body, 0)
        if step < STEPS - 1:
            e_pack(sim)

    def e_pack(sim):
        for i in range(2):
            SE[sim, i] = EF[e_row(sim, 1 + i, 0)]

    def halves(lo, hi):
        even = jnp.where(low, lo, pltpu.roll(hi, NZ, 1))
        odd = jnp.where(low, pltpu.roll(lo, NZ, 1), hi)
        return even, odd

    pl.semaphore_wait(barrier, len(partners))
    for sim in range(sims):
        for xt in range(X // 8):
            loads[sim, 0, xt].wait()

        def e_layout(a, carry):
            for c in range(3):
                even, odd = halves(ST[sim, c, a], ST[sim, c, a + T // 2])
                E[sim, c, 2 * a, 0:X, :] = even
                E[sim, c, 2 * a + 1, 0:X, :] = odd
            return carry

        lax.fori_loop(0, T // 2, e_layout, 0, unroll=4)
        e_pack(sim)
        e_send(sim)

    for c in perms:
        c.wait()

    def make_factor(a, carry):
        even, odd = halves(PS[a], PS[a + T // 2])
        fac[2 * a] = (COURANT * COURANT) / even
        fac[2 * a + 1] = (COURANT * COURANT) / odd
        return carry

    lax.fori_loop(0, T // 2, make_factor, 0, unroll=4)
    for sim in range(sims):
        for xt in range(X // 8):
            loads[sim, 1, xt].wait()

        def h_layout(a, carry):
            for c in range(3):
                even, odd = halves(ST[sim, 3 + c, a], ST[sim, 3 + c, a + T // 2])
                H[sim, c, 2 * a + 1, 8 : 8 + X, :] = even * (1.0 / COURANT)
                H[sim, c, 2 * a + 2, 8 : 8 + X, :] = odd * (1.0 / COURANT)
            return carry

        lax.fori_loop(0, T // 2, h_layout, 0, unroll=4)

    for step in range(STEPS):
        for sim in range(sims):
            e_arrive(sim)
            if step > 0:
                h_sent(sim)
            h_phase(sim)
            h_send(sim)
        for sim in range(sims):
            h_arrive(sim)
            e_sent(sim)
            e_phase(sim, step)
            if step < STEPS - 1:
                e_send(sim)
    for sim in range(sims):
        h_sent(sim)

    def d_layout(a, carry):
        PS[a], PS[a + T // 2] = halves(D[2 * a], D[2 * a + 1])
        return carry

    lax.fori_loop(0, T // 2, d_layout, 0, unroll=4)
    half = BX // 2
    for h in range(2):
        for p in range(X // BX):
            for xi in range(half):
                for yh in range(BY // 2):
                    j = xi * (BY // 2) + yh
                    start = yh * X + BX * p + half * h + xi
                    B[h, p * LBY : (p + 1) * LBY, j * 128 : (j + 1) * 128] = PS.reshape(
                        T * X, 128
                    )[pl.ds(start, LBY, stride=2 * X), :]
    peer = pltpu.make_async_remote_copy(
        B.at[1 - src], RB, src_sem.at[0], src_sem.at[1],
        device_id={"src": 1 - src}, device_id_type=MESH,
    )
    peer.start()
    peer.wait_recv()
    mine = B[src] + RB[...]
    routed = jnp.dot(OH1[...], split3(mine), preferred_element_type=jnp.float32)
    for o in range(n_gy):
        S2[o] = routed[o * cap : (o + 1) * cap, :]
    sends = []
    for d in range(1, n_gy):
        o = lax.rem(gy + d, n_gy)
        sends.append(
            pltpu.make_async_remote_copy(
                S2.at[o], R2.at[gy], rt_s.at[d], rt_r.at[d],
                device_id={"gy": o}, device_id_type=MESH,
            )
        )
        sends[-1].start()
    R2[gy] = S2[gy]
    for c in sends:
        c.wait_recv()
    for o in range(n_gy):
        RF[o * cap : (o + 1) * cap, :] = R2[o]
    out[...] = jnp.dot(OH2[...], split3(RF[...]), preferred_element_type=jnp.float32)
    for c in sends:
        c.wait_send()
    peer.wait_send()


def tiled(state):
    lead = state.shape[:-2]
    x, yz = state.shape[-2:]
    n = len(lead)
    state = state.reshape(lead + (x // 8, 8, yz // 128, 128))
    return state.transpose(tuple(range(n)) + (n, n + 2, n + 1, n + 3))


def per_device(
    n_gx, n_gy, forward_state, adjoint_state, permittivity, waveform, source_cell,
    block_owner, block_slot, owner_rows,
):
    NS = forward_state.shape[0]
    X, YZ = permittivity.shape
    T = YZ // 128
    NB = block_owner.shape[0] * block_owner.shape[1]
    cap = max(2, (NB + n_gy - 1) // n_gy)
    cols = BX * BY * NZ // 2
    sims = 2 * NS
    f32 = jnp.float32
    dma = pltpu.SemaphoreType.DMA
    any_spec = pl.BlockSpec(memory_space=pl.ANY)
    vmem = pl.BlockSpec(memory_space=pltpu.VMEM)
    return pl.pallas_call(
        functools.partial(kernel, n_gx, n_gy, cap),
        out_shape=jax.ShapeDtypeStruct((NB, cols), f32),
        in_specs=[any_spec] * 8,
        out_specs=vmem,
        scratch_shapes=[
            pltpu.VMEM((sims, 6, T, X, 128), f32),
            pltpu.VMEM((T, X, 128), f32),
            pltpu.VMEM((sims, 2, X, 128), f32),
            pltpu.VMEM((sims, 2, X, 128), f32),
            pltpu.VMEM((sims, 3, T + 1, X + 8, 128), f32),
            pltpu.VMEM((sims, 3, T + 1, X + 8, 128), f32),
            pltpu.VMEM((T, X, 128), f32),
            pltpu.VMEM((NS, 2, 3, T, X, 128), f32),
            pltpu.VMEM((NS, 3, T, X, 128), f32),
            pltpu.VMEM((T, X, 128), f32),
            pltpu.VMEM((sims, 2, T, 128), f32),
            pltpu.VMEM((sims, 2, T, 128), f32),
            pltpu.VMEM((sims, 2, T, 128), f32),
            pltpu.VMEM((sims, 2, T, 128), f32),
            pltpu.VMEM((2, NB, cols), f32),
            pltpu.VMEM((NB, cols), f32),
            pltpu.VMEM((n_gy, cap, cols), f32),
            pltpu.VMEM((n_gy, cap, cols), f32),
            pltpu.VMEM((n_gy * cap, cols), f32),
            pltpu.VMEM((NB, 3 * NB), jnp.bfloat16),
            pltpu.VMEM((NB, 3 * NB), jnp.bfloat16),
            pltpu.SMEM(waveform.shape, f32),
            pltpu.SMEM(source_cell.shape, jnp.int32),
            pltpu.VMEM(block_owner.shape, jnp.int32),
            pltpu.VMEM(block_slot.shape, jnp.int32),
            pltpu.VMEM(owner_rows.shape, jnp.int32),
            dma((5,)),
            dma((sims, 2, X // 8)),
            dma((X // 8,)),
            dma((sims,)),
            dma((sims,)),
            dma((sims,)),
            dma((sims,)),
            dma((sims, 2)),
            dma((sims, 2)),
            dma((sims, 2)),
            dma((sims, 2)),
            dma((2,)),
            dma((n_gy,)),
            dma((n_gy,)),
        ],
        compiler_params=pltpu.CompilerParams(
            collective_id=0, has_side_effects=True, vmem_limit_bytes=62 * 1024 * 1024
        ),
    )(
        tiled(forward_state), tiled(adjoint_state), tiled(permittivity),
        waveform, source_cell, block_owner, block_slot, owner_rows,
    )


def solution(mesh):
    in_specs = (
        P("src", None, "gx", "gy"),
        P("src", None, "gx", "gy"),
        P("gx", "gy"),
        P("src", None),
        P("src", None),
        P("gx", "gy"),
        P("gx", "gy"),
        P(("gx", "gy"), None),
    )
    out_specs = P(("gx", "gy"), "src")
    sizes = dict(mesh.shape)
    return jax.shard_map(
        functools.partial(per_device, sizes["gx"], sizes["gy"]),
        mesh=mesh, in_specs=in_specs, out_specs=out_specs, check_vma=False,
    )
```

```python
import functools

import jax
import jax.numpy as jnp
from jax import lax
from jax.experimental import pallas as pl
from jax.experimental.pallas import tpu as pltpu
from jax.sharding import PartitionSpec as P

NZ = 64
STEPS = 4
BX = 4
BY = 4
CHUNKS = 4
COURANT = 0.55
MESH = pl.DeviceIdType.MESH


def split3(v):
    hi = v.astype(jnp.bfloat16)
    rest = v - hi.astype(jnp.float32)
    mid = rest.astype(jnp.bfloat16)
    low = (rest - mid.astype(jnp.float32)).astype(jnp.bfloat16)
    return jnp.concatenate([hi, mid, low], axis=0)


def kernel(
    n_gx, n_gy, cap,
    fwd, adj, perm, wave_hbm, cell_hbm, owner_hbm, slot_hbm, rows_hbm, out,
    ST, PS, YE, YH, E, H, fac, inc, asv, D, SE, SH, GE, GH, B, RB, S2, R2, RF, OH1, OH2,
    wave, cell, owner, slot, rows, small_sem,
    load_sem, perm_sem,
    exs, exr, hxs, hxr, eys, eyr, hys, hyr, src_sem, rt_s, rt_r,
):
    T = fac.shape[0]
    X = fac.shape[1]
    NS = fwd.shape[0]
    NB = out.shape[0]
    sims = 2 * NS
    src = lax.axis_index("src")
    gx = lax.axis_index("gx")
    gy = lax.axis_index("gy")

    loads = {}
    for sim in range(sims):
        state = fwd if sim < NS else adj
        s = sim % NS
        for xt in range(X // 8):
            loads[sim, 0, xt] = pltpu.make_async_copy(
                state.at[s, pl.ds(0, 3), xt],
                ST.at[sim, pl.ds(0, 3), :, pl.ds(8 * xt, 8), :],
                load_sem.at[sim, 0, xt],
            )
            loads[sim, 1, xt] = pltpu.make_async_copy(
                state.at[s, pl.ds(3, 3), xt],
                ST.at[sim, pl.ds(3, 3), :, pl.ds(8 * xt, 8), :],
                load_sem.at[sim, 1, xt],
            )
    perms = [
        pltpu.make_async_copy(
            perm.at[xt], PS.at[:, pl.ds(8 * xt, 8), :], perm_sem.at[xt]
        )
        for xt in range(X // 8)
    ]
    for sim in range(sims):
        for xt in range(X // 8):
            loads[sim, 0, xt].start()
    for sim in range(sims):
        for xt in range(X // 8):
            loads[sim, 1, xt].start()
    smalls = [
        pltpu.make_async_copy(a, b, small_sem.at[i])
        for i, (a, b) in enumerate(
            (
                (wave_hbm, wave), (cell_hbm, cell), (owner_hbm, owner),
                (slot_hbm, slot), (rows_hbm, rows),
            )
        )
    ]
    for c in smalls:
        c.start()
    for c in perms:
        c.start()

    R = X + 8
    EF = E.reshape(sims * 3 * (T + 1) * R, 128)
    HF = H.reshape(sims * 3 * (T + 1) * R, 128)

    TC = T // CHUNKS

    def e_row(sim, c, r, t=0, n=TC):
        start = ((sim * 3 + c) * (T + 1) + t) * R + r
        return pl.ds(start, n, stride=R), slice(None)

    def h_row(sim, c, r, t=0, n=TC):
        return e_row(sim, c, r, t + 1, n)

    zero_tile = jnp.zeros((X, 128), jnp.float32)
    zero_rows = jnp.zeros((T, 128), jnp.float32)
    for sim in range(sims):
        for i in range(2):
            YE[sim, i] = zero_tile
            YH[sim, i] = zero_tile
            EF[e_row(sim, 1 + i, X, 0, T)] = zero_rows
            HF[h_row(sim, 1 + i, 7, 0, T)] = zero_rows

    barrier = pltpu.get_barrier_semaphore()
    partners = [
        {"gx": lax.rem(gx + 1, n_gx)},
        {"gx": lax.rem(gx + n_gx - 1, n_gx)},
        {"src": 1 - src},
    ]
    for d in range(1, n_gy):
        partners.append({"gy": lax.rem(gy + d, n_gy)})
    for device in partners:
        pl.semaphore_signal(barrier, inc=1, device_id=device, device_id_type=MESH)

    for c in smalls:
        c.wait()
    KB = 3 * NB
    LBY = owner.shape[1]
    dest = jnp.where(owner[...] >= 0, owner[...] * cap + slot[...], -1)
    dest = dest.astype(jnp.float32)
    q_i = lax.broadcasted_iota(jnp.int32, (LBY, KB), 0)
    b_i = lax.broadcasted_iota(jnp.int32, (LBY, KB), 1)
    pick = jnp.where(b_i % LBY == q_i, 1.0, 0.0)
    wide = jnp.dot(dest, pick, preferred_element_type=jnp.float32)
    p_i = lax.broadcasted_iota(jnp.int32, wide.shape, 0)
    l_i = lax.broadcasted_iota(jnp.int32, wide.shape, 1)
    line = jnp.sum(
        jnp.where((l_i % NB) // LBY == p_i, wide, 0.0), axis=0, keepdims=True
    )
    r_f = lax.broadcasted_iota(jnp.int32, (NB, KB), 0).astype(jnp.float32)
    OH1[...] = jnp.where(line == r_f, 1.0, 0.0).astype(jnp.bfloat16)
    m_i = lax.broadcasted_iota(jnp.int32, (NB, KB), 0)
    k_i = lax.broadcasted_iota(jnp.int32, (NB, KB), 1)
    pick = jnp.where(k_i % NB == m_i, 1.0, 0.0)
    row8 = jnp.broadcast_to(rows[...].astype(jnp.float32), (8, NB))
    line = jnp.dot(row8, pick, preferred_element_type=jnp.float32)[0:1, :]
    OH2[...] = jnp.where(line == r_f, 1.0, 0.0).astype(jnp.bfloat16)

    lane = lax.broadcasted_iota(jnp.int32, (X, 128), 1)
    row = lax.broadcasted_iota(jnp.int32, (X, 128), 0)
    z = lane % NZ
    z_first = z == 0
    z_last = z == NZ - 1
    low = lane < NZ
    cells_yz = T * 128
    linear = row * cells_yz + jnp.where(low, z, z + T * NZ)

    def e_x(sim, q):
        return pltpu.make_async_remote_copy(
            SE.at[sim, q], GE.at[sim, q], exs.at[sim, q], exr.at[sim, q],
            device_id={"gx": gx - 1}, device_id_type=MESH,
        )

    def h_x(sim, q):
        return pltpu.make_async_remote_copy(
            SH.at[sim, q], GH.at[sim, q], hxs.at[sim, q], hxr.at[sim, q],
            device_id={"gx": gx + 1}, device_id_type=MESH,
        )

    def e_ys(sim):
        return [
            pltpu.make_async_remote_copy(
                E.at[sim, c, 0, pl.ds(0, X), :],
                YE.at[sim, i],
                eys.at[sim, i], eyr.at[sim, i],
                device_id={"gy": gy - 1}, device_id_type=MESH,
            )
            for i, c in enumerate((0, 2))
        ]

    def h_ys(sim):
        return [
            pltpu.make_async_remote_copy(
                H.at[sim, c, T, pl.ds(8, X), :],
                YH.at[sim, i],
                hys.at[sim, i], hyr.at[sim, i],
                device_id={"gy": gy + 1}, device_id_type=MESH,
            )
            for i, c in enumerate((0, 2))
        ]

    down_x, up_x = gx > 0, gx < n_gx - 1
    down_y, up_y = gy > 0, gy < n_gy - 1

    def e_send_x(sim, q):
        for i in range(2):
            SE[sim, q, i] = EF[e_row(sim, 1 + i, 0, q * TC)]

        @pl.when(down_x)
        def _():
            e_x(sim, q).start()

    def h_send_x(sim, q):
        for i in range(2):
            SH[sim, q, i] = HF[h_row(sim, 1 + i, 7 + X, q * TC)]

        @pl.when(up_x)
        def _():
            h_x(sim, q).start()

    def e_send_y(sim):
        @pl.when(down_y)
        def _():
            for y in e_ys(sim):
                y.start()

    def h_send_y(sim):
        @pl.when(up_y)
        def _():
            for y in h_ys(sim):
                y.start()

    def e_sent(sim):
        @pl.when(down_x)
        def _():
            for q in range(CHUNKS):
                e_x(sim, q).wait_send()

        @pl.when(down_y)
        def _():
            for y in e_ys(sim):
                y.wait_send()

    def h_sent(sim):
        @pl.when(up_x)
        def _():
            for q in range(CHUNKS):
                h_x(sim, q).wait_send()

        @pl.when(up_y)
        def _():
            for y in h_ys(sim):
                y.wait_send()

    def e_arrive_x(sim, q):
        @pl.when(up_x)
        def _():
            e_x(sim, q).wait_recv()
            for i in range(2):
                EF[e_row(sim, 1 + i, X, q * TC)] = GE[sim, q, i]

    def h_arrive_x(sim, q):
        @pl.when(down_x)
        def _():
            h_x(sim, q).wait_recv()
            for i in range(2):
                HF[h_row(sim, 1 + i, 7, q * TC)] = GH[sim, q, i]

    def e_arrive_y(sim):
        @pl.when(up_y)
        def _():
            for y in e_ys(sim):
                y.wait_recv()

        for i, c in enumerate((0, 2)):
            edge = jnp.where(low, YE[sim, i], E[sim, c, 0, 0:X, :])
            E[sim, c, T, 0:X, :] = pltpu.roll(edge, NZ, 1)

    def h_arrive_y(sim):
        @pl.when(down_y)
        def _():
            for y in h_ys(sim):
                y.wait_recv()

        for i, c in enumerate((0, 2)):
            edge = jnp.where(low, H[sim, c, T, 8 : 8 + X, :], YH[sim, i])
            H[sim, c, 0, 8 : 8 + X, :] = pltpu.roll(edge, NZ, 1)

    def h_phase(sim):
        def tile(t, held):
            ex, ez = held
            ey = E[sim, 1, t, 0:X, :]
            exn = E[sim, 0, t + 1, 0:X, :]
            ezn = E[sim, 2, t + 1, 0:X, :]
            eyx = E[sim, 1, t, 1 : X + 1, :]
            ezx = E[sim, 2, t, 1 : X + 1, :]
            exz = jnp.where(z_last, 0.0, pltpu.roll(ex, 127, 1))
            eyz = jnp.where(z_last, 0.0, pltpu.roll(ey, 127, 1))
            hx = H[sim, 0, t + 1, 8 : 8 + X, :]
            hy = H[sim, 1, t + 1, 8 : 8 + X, :]
            hz = H[sim, 2, t + 1, 8 : 8 + X, :]
            hx = hx - ((ezn - ez) - (eyz - ey))
            hy = hy - ((exz - ex) - (ezx - ez))
            hz = hz - ((eyx - ey) - (exn - ex))
            H[sim, 0, t + 1, 8 : 8 + X, :] = hx
            H[sim, 1, t + 1, 8 : 8 + X, :] = hy
            H[sim, 2, t + 1, 8 : 8 + X, :] = hz
            return exn, ezn

        def body(i, carry):
            q = lax.rem(i + CHUNKS - 1, CHUNKS)
            e_arrive_x(sim, q)
            t = q * TC
            held = E[sim, 0, t, 0:X, :], E[sim, 2, t, 0:X, :]
            for k in range(TC):
                held = tile(t + k, held)
            h_send_x(sim, q)

            @pl.when(i == 0)
            def _():
                h_send_y(sim)

            return carry

        lax.fori_loop(0, CHUNKS, body, 0)

    def e_phase(sim, step):
        s = sim % NS
        forward = sim < NS
        if forward:
            lx = cell[s, 0] - gx * X
            lyz = (cell[s, 1] - gy * (cells_yz // NZ)) * NZ + cell[s, 2]
            inside = (lx >= 0) & (lx < X) & (lyz >= 0) & (lyz < cells_yz)
            target = jnp.where(inside, lx * cells_yz + lyz, -1)
            pulse = wave[s, step]

        def tile(t, held):
            hxp, hzp = held
            hx = H[sim, 0, t + 1, 8 : 8 + X, :]
            hy = H[sim, 1, t + 1, 8 : 8 + X, :]
            hz = H[sim, 2, t + 1, 8 : 8 + X, :]
            hyx = H[sim, 1, t + 1, 7 : 7 + X, :]
            hzx = H[sim, 2, t + 1, 7 : 7 + X, :]
            hxz = jnp.where(z_first, 0.0, pltpu.roll(hx, 1, 1))
            hyz = jnp.where(z_first, 0.0, pltpu.roll(hy, 1, 1))
            f = fac[t]
            d0 = f * ((hz - hzp) - (hy - hyz))
            d1 = f * ((hx - hxz) - (hz - hzx))
            d2 = f * ((hy - hyx) - (hx - hxp))
            if forward:
                hit = linear == target - t * NZ
                d2 = d2 + jnp.where(hit, pulse, 0.0)
            if not (forward and step == STEPS - 1):
                e0 = E[sim, 0, t, 0:X, :] + d0
                e1 = E[sim, 1, t, 0:X, :] + d1
                e2 = E[sim, 2, t, 0:X, :] + d2
            if step < STEPS - 1:
                E[sim, 0, t, 0:X, :] = e0
                E[sim, 1, t, 0:X, :] = e1
                E[sim, 2, t, 0:X, :] = e2
            if forward:
                if step < 2:
                    inc[s, step, 0, t] = d0
                    inc[s, step, 1, t] = d1
                    inc[s, step, 2, t] = d2
                else:
                    if step == 2:
                        a = [E[NS + s, c, t, 0:X, :] for c in range(3)]
                    else:
                        a = [asv[s, c, t] for c in range(3)]
                    term = d0 * a[0] + d1 * a[1] + d2 * a[2]
                    if step == 2 and s == 0:
                        D[t] = term
                    else:
                        D[t] = D[t] + term
            else:
                if step == 0:
                    asv[s, 0, t] = e0
                    asv[s, 1, t] = e1
                    asv[s, 2, t] = e2
                elif step >= 2:
                    k = STEPS - 1 - step
                    total = D[t] + (
                        e0 * inc[s, k, 0, t] + e1 * inc[s, k, 1, t] + e2 * inc[s, k, 2, t]
                    )
                    if step == STEPS - 1 and s == NS - 1:
                        total = total * (f * (-1.0 / (COURANT * COURANT)))
                    D[t] = total
            return hx, hz

        def body(i, carry):
            q = lax.rem(CHUNKS - i, CHUNKS)
            h_arrive_x(sim, q)
            t = q * TC
            held = H[sim, 0, t, 8 : 8 + X, :], H[sim, 2, t, 8 : 8 + X, :]
            for k in range(TC):
                held = tile(t + k, held)
            if step < STEPS - 1:
                e_send_x(sim, q)

                @pl.when(i == 0)
                def _():
                    e_send_y(sim)

            return carry

        lax.fori_loop(0, CHUNKS, body, 0)

    def halves(lo, hi):
        even = jnp.where(low, lo, pltpu.roll(hi, NZ, 1))
        odd = jnp.where(low, pltpu.roll(lo, NZ, 1), hi)
        return even, odd

    pl.semaphore_wait(barrier, len(partners))
    for sim in range(sims):
        for xt in range(X // 8):
            loads[sim, 0, xt].wait()

        def e_layout(a, carry):
            for c in range(3):
                even, odd = halves(ST[sim, c, a], ST[sim, c, a + T // 2])
                E[sim, c, 2 * a, 0:X, :] = even
                E[sim, c, 2 * a + 1, 0:X, :] = odd
            return carry

        lax.fori_loop(0, T // 2, e_layout, 0, unroll=4)
        e_send_y(sim)
        for i in range(CHUNKS):
            e_send_x(sim, (CHUNKS - i) % CHUNKS)

    for c in perms:
        c.wait()

    def make_factor(a, carry):
        even, odd = halves(PS[a], PS[a + T // 2])
        fac[2 * a] = (COURANT * COURANT) / even
        fac[2 * a + 1] = (COURANT * COURANT) / odd
        return carry

    lax.fori_loop(0, T // 2, make_factor, 0, unroll=4)

    def h_load(sim):
        for xt in range(X // 8):
            loads[sim, 1, xt].wait()

        def h_layout(a, carry):
            for c in range(3):
                even, odd = halves(ST[sim, 3 + c, a], ST[sim, 3 + c, a + T // 2])
                H[sim, c, 2 * a + 1, 8 : 8 + X, :] = even * (1.0 / COURANT)
                H[sim, c, 2 * a + 2, 8 : 8 + X, :] = odd * (1.0 / COURANT)
            return carry

        lax.fori_loop(0, T // 2, h_layout, 0, unroll=4)

    for step in range(STEPS):
        for sim in range(sims):
            if step == 0:
                h_load(sim)
            else:
                h_sent(sim)
            e_arrive_y(sim)
            h_phase(sim)
        for sim in range(sims):
            h_arrive_y(sim)
            e_sent(sim)
            e_phase(sim, step)
    for sim in range(sims):
        h_sent(sim)

    def d_layout(a, carry):
        PS[a], PS[a + T // 2] = halves(D[2 * a], D[2 * a + 1])
        return carry

    lax.fori_loop(0, T // 2, d_layout, 0, unroll=4)
    half = BX // 2
    for h in range(2):
        for p in range(X // BX):
            for xi in range(half):
                for yh in range(BY // 2):
                    j = xi * (BY // 2) + yh
                    start = yh * X + BX * p + half * h + xi
                    B[h, p * LBY : (p + 1) * LBY, j * 128 : (j + 1) * 128] = PS.reshape(
                        T * X, 128
                    )[pl.ds(start, LBY, stride=2 * X), :]
    peer = pltpu.make_async_remote_copy(
        B.at[1 - src], RB, src_sem.at[0], src_sem.at[1],
        device_id={"src": 1 - src}, device_id_type=MESH,
    )
    peer.start()
    peer.wait_recv()
    mine = B[src] + RB[...]
    routed = jnp.dot(OH1[...], split3(mine), preferred_element_type=jnp.float32)
    for o in range(n_gy):
        S2[o] = routed[o * cap : (o + 1) * cap, :]
    sends = []
    for d in range(1, n_gy):
        o = lax.rem(gy + d, n_gy)
        sends.append(
            pltpu.make_async_remote_copy(
                S2.at[o], R2.at[gy], rt_s.at[d], rt_r.at[d],
                device_id={"gy": o}, device_id_type=MESH,
            )
        )
        sends[-1].start()
    R2[gy] = S2[gy]
    for c in sends:
        c.wait_recv()
    for o in range(n_gy):
        RF[o * cap : (o + 1) * cap, :] = R2[o]
    out[...] = jnp.dot(OH2[...], split3(RF[...]), preferred_element_type=jnp.float32)
    for c in sends:
        c.wait_send()
    peer.wait_send()


def tiled(state):
    lead = state.shape[:-2]
    x, yz = state.shape[-2:]
    n = len(lead)
    state = state.reshape(lead + (x // 8, 8, yz // 128, 128))
    return state.transpose(tuple(range(n)) + (n, n + 2, n + 1, n + 3))


def per_device(
    n_gx, n_gy, forward_state, adjoint_state, permittivity, waveform, source_cell,
    block_owner, block_slot, owner_rows,
):
    NS = forward_state.shape[0]
    X, YZ = permittivity.shape
    T = YZ // 128
    NB = block_owner.shape[0] * block_owner.shape[1]
    cap = max(2, (NB + n_gy - 1) // n_gy)
    cols = BX * BY * NZ // 2
    sims = 2 * NS
    f32 = jnp.float32
    dma = pltpu.SemaphoreType.DMA
    any_spec = pl.BlockSpec(memory_space=pl.ANY)
    vmem = pl.BlockSpec(memory_space=pltpu.VMEM)
    return pl.pallas_call(
        functools.partial(kernel, n_gx, n_gy, cap),
        out_shape=jax.ShapeDtypeStruct((NB, cols), f32),
        in_specs=[any_spec] * 8,
        out_specs=vmem,
        scratch_shapes=[
            pltpu.VMEM((sims, 6, T, X, 128), f32),
            pltpu.VMEM((T, X, 128), f32),
            pltpu.VMEM((sims, 2, X, 128), f32),
            pltpu.VMEM((sims, 2, X, 128), f32),
            pltpu.VMEM((sims, 3, T + 1, X + 8, 128), f32),
            pltpu.VMEM((sims, 3, T + 1, X + 8, 128), f32),
            pltpu.VMEM((T, X, 128), f32),
            pltpu.VMEM((NS, 2, 3, T, X, 128), f32),
            pltpu.VMEM((NS, 3, T, X, 128), f32),
            pltpu.VMEM((T, X, 128), f32),
            pltpu.VMEM((sims, CHUNKS, 2, T // CHUNKS, 128), f32),
            pltpu.VMEM((sims, CHUNKS, 2, T // CHUNKS, 128), f32),
            pltpu.VMEM((sims, CHUNKS, 2, T // CHUNKS, 128), f32),
            pltpu.VMEM((sims, CHUNKS, 2, T // CHUNKS, 128), f32),
            pltpu.VMEM((2, NB, cols), f32),
            pltpu.VMEM((NB, cols), f32),
            pltpu.VMEM((n_gy, cap, cols), f32),
            pltpu.VMEM((n_gy, cap, cols), f32),
            pltpu.VMEM((n_gy * cap, cols), f32),
            pltpu.VMEM((NB, 3 * NB), jnp.bfloat16),
            pltpu.VMEM((NB, 3 * NB), jnp.bfloat16),
            pltpu.SMEM(waveform.shape, f32),
            pltpu.SMEM(source_cell.shape, jnp.int32),
            pltpu.VMEM(block_owner.shape, jnp.int32),
            pltpu.VMEM(block_slot.shape, jnp.int32),
            pltpu.VMEM(owner_rows.shape, jnp.int32),
            dma((5,)),
            dma((sims, 2, X // 8)),
            dma((X // 8,)),
            dma((sims, CHUNKS)),
            dma((sims, CHUNKS)),
            dma((sims, CHUNKS)),
            dma((sims, CHUNKS)),
            dma((sims, 2)),
            dma((sims, 2)),
            dma((sims, 2)),
            dma((sims, 2)),
            dma((2,)),
            dma((n_gy,)),
            dma((n_gy,)),
        ],
        compiler_params=pltpu.CompilerParams(
            collective_id=0, has_side_effects=True, vmem_limit_bytes=62 * 1024 * 1024
        ),
    )(
        tiled(forward_state), tiled(adjoint_state), tiled(permittivity),
        waveform, source_cell, block_owner, block_slot, owner_rows,
    )


def solution(mesh):
    in_specs = (
        P("src", None, "gx", "gy"),
        P("src", None, "gx", "gy"),
        P("gx", "gy"),
        P("src", None),
        P("src", None),
        P("gx", "gy"),
        P("gx", "gy"),
        P(("gx", "gy"), None),
    )
    out_specs = P(("gx", "gy"), "src")
    sizes = dict(mesh.shape)
    return jax.shard_map(
        functools.partial(per_device, sizes["gx"], sizes["gy"]),
        mesh=mesh, in_specs=in_specs, out_specs=out_specs, check_vma=False,
    )
```

```python
import functools

import jax
import jax.numpy as jnp
from jax import lax
from jax.experimental import pallas as pl
from jax.experimental.pallas import tpu as pltpu
from jax.sharding import PartitionSpec as P

NZ = 64
STEPS = 4
BX = 4
BY = 4
CHUNKS = 4
COURANT = 0.55
MESH = pl.DeviceIdType.MESH


def split3(v):
    hi = v.astype(jnp.bfloat16)
    rest = v - hi.astype(jnp.float32)
    mid = rest.astype(jnp.bfloat16)
    low = (rest - mid.astype(jnp.float32)).astype(jnp.bfloat16)
    return jnp.concatenate([hi, mid, low], axis=0)


def kernel(
    n_gx, n_gy, cap,
    fwd, adj, perm, wave_hbm, cell_hbm, owner_hbm, slot_hbm, rows_hbm, out,
    ST, PS, YE, YH, E, H, fac, inc, asv, D, SE, SH, GE, GH, B, RB, S2, R2, RF, OH1, OH2,
    wave, cell, owner, slot, rows, small_sem,
    load_sem, perm_sem,
    exs, exr, hxs, hxr, eys, eyr, hys, hyr, src_sem, rt_s, rt_r,
):
    T = fac.shape[0]
    X = fac.shape[1]
    NS = fwd.shape[0]
    NB = out.shape[0]
    sims = 2 * NS
    src = lax.axis_index("src")
    gx = lax.axis_index("gx")
    gy = lax.axis_index("gy")

    loads = {}
    for sim in range(sims):
        state = fwd if sim < NS else adj
        s = sim % NS
        for xt in range(X // 8):
            loads[sim, 0, xt] = pltpu.make_async_copy(
                state.at[s, pl.ds(0, 3), xt],
                ST.at[sim, pl.ds(0, 3), :, pl.ds(8 * xt, 8), :],
                load_sem.at[sim, 0, xt],
            )
            loads[sim, 1, xt] = pltpu.make_async_copy(
                state.at[s, pl.ds(3, 3), xt],
                ST.at[sim, pl.ds(3, 3), :, pl.ds(8 * xt, 8), :],
                load_sem.at[sim, 1, xt],
            )
    perms = [
        pltpu.make_async_copy(
            perm.at[xt], PS.at[:, pl.ds(8 * xt, 8), :], perm_sem.at[xt]
        )
        for xt in range(X // 8)
    ]
    for sim in range(sims):
        for xt in range(X // 8):
            loads[sim, 0, xt].start()
    for sim in range(sims):
        for xt in range(X // 8):
            loads[sim, 1, xt].start()
    smalls = [
        pltpu.make_async_copy(a, b, small_sem.at[i])
        for i, (a, b) in enumerate(
            (
                (wave_hbm, wave), (cell_hbm, cell), (owner_hbm, owner),
                (slot_hbm, slot), (rows_hbm, rows),
            )
        )
    ]
    for c in smalls:
        c.start()
    for c in perms:
        c.start()

    R = X + 8
    EF = E.reshape(sims * 3 * (T + 1) * R, 128)
    HF = H.reshape(sims * 3 * (T + 1) * R, 128)

    TC = T // CHUNKS

    def e_row(sim, c, r, t=0, n=TC):
        start = ((sim * 3 + c) * (T + 1) + t) * R + r
        return pl.ds(start, n, stride=R), slice(None)

    def h_row(sim, c, r, t=0, n=TC):
        return e_row(sim, c, r, t + 1, n)

    zero_tile = jnp.zeros((X, 128), jnp.float32)
    zero_rows = jnp.zeros((T, 128), jnp.float32)
    for sim in range(sims):
        for i in range(2):
            YE[sim, i] = zero_tile
            YH[sim, i] = zero_tile
            EF[e_row(sim, 1 + i, X, 0, T)] = zero_rows
            HF[h_row(sim, 1 + i, 7, 0, T)] = zero_rows

    barrier = pltpu.get_barrier_semaphore()
    partners = [
        {"gx": lax.rem(gx + 1, n_gx)},
        {"gx": lax.rem(gx + n_gx - 1, n_gx)},
        {"src": 1 - src},
    ]
    for d in range(1, n_gy):
        partners.append({"gy": lax.rem(gy + d, n_gy)})
    for device in partners:
        pl.semaphore_signal(barrier, inc=1, device_id=device, device_id_type=MESH)

    for c in smalls:
        c.wait()
    KB = 3 * NB
    LBY = owner.shape[1]
    dest = jnp.where(owner[...] >= 0, owner[...] * cap + slot[...], -1)
    dest = dest.astype(jnp.float32)
    q_i = lax.broadcasted_iota(jnp.int32, (LBY, KB), 0)
    b_i = lax.broadcasted_iota(jnp.int32, (LBY, KB), 1)
    pick = jnp.where(b_i % LBY == q_i, 1.0, 0.0)
    wide = jnp.dot(dest, pick, preferred_element_type=jnp.float32)
    p_i = lax.broadcasted_iota(jnp.int32, wide.shape, 0)
    l_i = lax.broadcasted_iota(jnp.int32, wide.shape, 1)
    line = jnp.sum(
        jnp.where((l_i % NB) // LBY == p_i, wide, 0.0), axis=0, keepdims=True
    )
    r_f = lax.broadcasted_iota(jnp.int32, (NB, KB), 0).astype(jnp.float32)
    OH1[...] = jnp.where(line == r_f, 1.0, 0.0).astype(jnp.bfloat16)
    m_i = lax.broadcasted_iota(jnp.int32, (NB, KB), 0)
    k_i = lax.broadcasted_iota(jnp.int32, (NB, KB), 1)
    pick = jnp.where(k_i % NB == m_i, 1.0, 0.0)
    row8 = jnp.broadcast_to(rows[...].astype(jnp.float32), (8, NB))
    line = jnp.dot(row8, pick, preferred_element_type=jnp.float32)[0:1, :]
    OH2[...] = jnp.where(line == r_f, 1.0, 0.0).astype(jnp.bfloat16)

    lane = lax.broadcasted_iota(jnp.int32, (X, 128), 1)
    row = lax.broadcasted_iota(jnp.int32, (X, 128), 0)
    z = lane % NZ
    z_first = z == 0
    z_last = z == NZ - 1
    low = lane < NZ
    cells_yz = T * 128
    linear = row * cells_yz + jnp.where(low, z, z + T * NZ)

    def e_x(sim, q):
        return pltpu.make_async_remote_copy(
            SE.at[sim, q], GE.at[sim, q], exs.at[sim, q], exr.at[sim, q],
            device_id={"gx": gx - 1}, device_id_type=MESH,
        )

    def h_x(sim, q):
        return pltpu.make_async_remote_copy(
            SH.at[sim, q], GH.at[sim, q], hxs.at[sim, q], hxr.at[sim, q],
            device_id={"gx": gx + 1}, device_id_type=MESH,
        )

    def e_ys(sim):
        return [
            pltpu.make_async_remote_copy(
                E.at[sim, c, 0, pl.ds(0, X), :],
                YE.at[sim, i],
                eys.at[sim, i], eyr.at[sim, i],
                device_id={"gy": gy - 1}, device_id_type=MESH,
            )
            for i, c in enumerate((0, 2))
        ]

    def h_ys(sim):
        return [
            pltpu.make_async_remote_copy(
                H.at[sim, c, T, pl.ds(8, X), :],
                YH.at[sim, i],
                hys.at[sim, i], hyr.at[sim, i],
                device_id={"gy": gy + 1}, device_id_type=MESH,
            )
            for i, c in enumerate((0, 2))
        ]

    down_x, up_x = gx > 0, gx < n_gx - 1
    down_y, up_y = gy > 0, gy < n_gy - 1

    def e_send_x(sim, q):
        for i in range(2):
            SE[sim, q, i] = EF[e_row(sim, 1 + i, 0, q * TC)]

        @pl.when(down_x)
        def _():
            e_x(sim, q).start()

    def h_send_x(sim, q):
        for i in range(2):
            SH[sim, q, i] = HF[h_row(sim, 1 + i, 7 + X, q * TC)]

        @pl.when(up_x)
        def _():
            h_x(sim, q).start()

    def e_send_y(sim):
        @pl.when(down_y)
        def _():
            for y in e_ys(sim):
                y.start()

    def h_send_y(sim):
        @pl.when(up_y)
        def _():
            for y in h_ys(sim):
                y.start()

    def e_sent(sim):
        @pl.when(down_x)
        def _():
            for q in range(CHUNKS):
                e_x(sim, q).wait_send()

        @pl.when(down_y)
        def _():
            for y in e_ys(sim):
                y.wait_send()

    def h_sent(sim):
        @pl.when(up_x)
        def _():
            for q in range(CHUNKS):
                h_x(sim, q).wait_send()

        @pl.when(up_y)
        def _():
            for y in h_ys(sim):
                y.wait_send()

    def e_arrive_x(sim, q):
        @pl.when(up_x)
        def _():
            e_x(sim, q).wait_recv()
            for i in range(2):
                EF[e_row(sim, 1 + i, X, q * TC)] = GE[sim, q, i]

    def h_arrive_x(sim, q):
        @pl.when(down_x)
        def _():
            h_x(sim, q).wait_recv()
            for i in range(2):
                HF[h_row(sim, 1 + i, 7, q * TC)] = GH[sim, q, i]

    def e_arrive_y(sim):
        @pl.when(up_y)
        def _():
            for y in e_ys(sim):
                y.wait_recv()

        for i, c in enumerate((0, 2)):
            edge = jnp.where(low, YE[sim, i], E[sim, c, 0, 0:X, :])
            E[sim, c, T, 0:X, :] = pltpu.roll(edge, NZ, 1)

    def h_arrive_y(sim):
        @pl.when(down_y)
        def _():
            for y in h_ys(sim):
                y.wait_recv()

        for i, c in enumerate((0, 2)):
            edge = jnp.where(low, H[sim, c, T, 8 : 8 + X, :], YH[sim, i])
            H[sim, c, 0, 8 : 8 + X, :] = pltpu.roll(edge, NZ, 1)

    def h_phase(sim):
        def tile(t, held):
            ex, ez = held
            ey = E[sim, 1, t, 0:X, :]
            exn = E[sim, 0, t + 1, 0:X, :]
            ezn = E[sim, 2, t + 1, 0:X, :]
            eyx = E[sim, 1, t, 1 : X + 1, :]
            ezx = E[sim, 2, t, 1 : X + 1, :]
            exz = jnp.where(z_last, 0.0, pltpu.roll(ex, 127, 1))
            eyz = jnp.where(z_last, 0.0, pltpu.roll(ey, 127, 1))
            hx = H[sim, 0, t + 1, 8 : 8 + X, :]
            hy = H[sim, 1, t + 1, 8 : 8 + X, :]
            hz = H[sim, 2, t + 1, 8 : 8 + X, :]
            hx = hx - ((ezn - ez) - (eyz - ey))
            hy = hy - ((exz - ex) - (ezx - ez))
            hz = hz - ((eyx - ey) - (exn - ex))
            H[sim, 0, t + 1, 8 : 8 + X, :] = hx
            H[sim, 1, t + 1, 8 : 8 + X, :] = hy
            H[sim, 2, t + 1, 8 : 8 + X, :] = hz
            return exn, ezn

        def body(i, carry):
            q = lax.rem(i + CHUNKS - 1, CHUNKS)
            e_arrive_x(sim, q)
            t = q * TC
            held = E[sim, 0, t, 0:X, :], E[sim, 2, t, 0:X, :]
            for k in range(TC):
                held = tile(t + k, held)
            h_send_x(sim, q)

            @pl.when(i == 0)
            def _():
                h_send_y(sim)

            return carry

        lax.fori_loop(0, CHUNKS, body, 0)

    def e_phase(sim, step, forward, s):
        if forward:
            lx = cell[s, 0] - gx * X
            lyz = (cell[s, 1] - gy * (cells_yz // NZ)) * NZ + cell[s, 2]
            inside = (lx >= 0) & (lx < X) & (lyz >= 0) & (lyz < cells_yz)
            target = jnp.where(inside, lx * cells_yz + lyz, -1)
            pulse = wave[s, step]

        def tile(t, held):
            hxp, hzp = held
            hx = H[sim, 0, t + 1, 8 : 8 + X, :]
            hy = H[sim, 1, t + 1, 8 : 8 + X, :]
            hz = H[sim, 2, t + 1, 8 : 8 + X, :]
            hyx = H[sim, 1, t + 1, 7 : 7 + X, :]
            hzx = H[sim, 2, t + 1, 7 : 7 + X, :]
            hxz = jnp.where(z_first, 0.0, pltpu.roll(hx, 1, 1))
            hyz = jnp.where(z_first, 0.0, pltpu.roll(hy, 1, 1))
            f = fac[t]
            d0 = f * ((hz - hzp) - (hy - hyz))
            d1 = f * ((hx - hxz) - (hz - hzx))
            d2 = f * ((hy - hyx) - (hx - hxp))
            if forward:
                hit = linear == target - t * NZ
                d2 = d2 + jnp.where(hit, pulse, 0.0)
            if not (forward and step == STEPS - 1):
                e0 = E[sim, 0, t, 0:X, :] + d0
                e1 = E[sim, 1, t, 0:X, :] + d1
                e2 = E[sim, 2, t, 0:X, :] + d2
            if step < STEPS - 1:
                E[sim, 0, t, 0:X, :] = e0
                E[sim, 1, t, 0:X, :] = e1
                E[sim, 2, t, 0:X, :] = e2
            if forward:
                if step < 2:
                    inc[s, step, 0, t] = d0
                    inc[s, step, 1, t] = d1
                    inc[s, step, 2, t] = d2
                else:
                    if step == 2:
                        a = [E[NS + s, c, t, 0:X, :] for c in range(3)]
                    else:
                        a = [asv[s, c, t] for c in range(3)]
                    term = d0 * a[0] + d1 * a[1] + d2 * a[2]
                    D[t] = D[t] + term
            else:
                if step == 0:
                    asv[s, 0, t] = e0
                    asv[s, 1, t] = e1
                    asv[s, 2, t] = e2
                elif step >= 2:
                    k = STEPS - 1 - step
                    total = D[t] + (
                        e0 * inc[s, k, 0, t] + e1 * inc[s, k, 1, t] + e2 * inc[s, k, 2, t]
                    )
                    D[t] = total
            return hx, hz

        def body(i, carry):
            q = lax.rem(CHUNKS - i, CHUNKS)
            h_arrive_x(sim, q)
            t = q * TC
            held = H[sim, 0, t, 8 : 8 + X, :], H[sim, 2, t, 8 : 8 + X, :]
            for k in range(TC):
                held = tile(t + k, held)
            if step < STEPS - 1:
                e_send_x(sim, q)

                @pl.when(i == 0)
                def _():
                    e_send_y(sim)

            return carry

        lax.fori_loop(0, CHUNKS, body, 0)

    def halves(lo, hi):
        even = jnp.where(low, lo, pltpu.roll(hi, NZ, 1))
        odd = jnp.where(low, pltpu.roll(lo, NZ, 1), hi)
        return even, odd

    pl.semaphore_wait(barrier, len(partners))
    for sim in range(sims):
        for xt in range(X // 8):
            loads[sim, 0, xt].wait()

        def e_layout(a, carry):
            for c in range(3):
                even, odd = halves(ST[sim, c, a], ST[sim, c, a + T // 2])
                E[sim, c, 2 * a, 0:X, :] = even
                E[sim, c, 2 * a + 1, 0:X, :] = odd
            return carry

        lax.fori_loop(0, T // 2, e_layout, 0, unroll=4)
        e_send_y(sim)
        for i in range(CHUNKS):
            e_send_x(sim, (CHUNKS - i) % CHUNKS)

    for c in perms:
        c.wait()

    def make_factor(a, carry):
        even, odd = halves(PS[a], PS[a + T // 2])
        fac[2 * a] = (COURANT * COURANT) / even
        fac[2 * a + 1] = (COURANT * COURANT) / odd
        D[2 * a] = zero_tile
        D[2 * a + 1] = zero_tile
        return carry

    lax.fori_loop(0, T // 2, make_factor, 0, unroll=4)

    def h_load(sim):
        for xt in range(X // 8):
            loads[sim, 1, xt].wait()

        def h_layout(a, carry):
            for c in range(3):
                even, odd = halves(ST[sim, 3 + c, a], ST[sim, 3 + c, a + T // 2])
                H[sim, c, 2 * a + 1, 8 : 8 + X, :] = even * (1.0 / COURANT)
                H[sim, c, 2 * a + 2, 8 : 8 + X, :] = odd * (1.0 / COURANT)
            return carry

        lax.fori_loop(0, T // 2, h_layout, 0, unroll=4)

    for step in range(STEPS):
        for sim in range(sims):
            if step == 0:
                h_load(sim)

        def h_run(sim, carry):
            if step > 0:
                h_sent(sim)
            e_arrive_y(sim)
            h_phase(sim)
            return carry

        def e_run(forward, s, carry):
            sim = s if forward else s + NS
            h_arrive_y(sim)
            e_sent(sim)
            e_phase(sim, step, forward, s)
            return carry

        lax.fori_loop(0, sims, h_run, 0)
        lax.fori_loop(0, NS, functools.partial(e_run, True), 0)
        lax.fori_loop(0, NS, functools.partial(e_run, False), 0)
    for sim in range(sims):
        h_sent(sim)

    scale = -1.0 / (COURANT * COURANT)

    def d_layout(a, carry):
        PS[a], PS[a + T // 2] = halves(
            D[2 * a] * (fac[2 * a] * scale), D[2 * a + 1] * (fac[2 * a + 1] * scale)
        )
        return carry

    lax.fori_loop(0, T // 2, d_layout, 0, unroll=4)
    half = BX // 2
    for h in range(2):
        for p in range(X // BX):
            for xi in range(half):
                for yh in range(BY // 2):
                    j = xi * (BY // 2) + yh
                    start = yh * X + BX * p + half * h + xi
                    B[h, p * LBY : (p + 1) * LBY, j * 128 : (j + 1) * 128] = PS.reshape(
                        T * X, 128
                    )[pl.ds(start, LBY, stride=2 * X), :]
    peer = pltpu.make_async_remote_copy(
        B.at[1 - src], RB, src_sem.at[0], src_sem.at[1],
        device_id={"src": 1 - src}, device_id_type=MESH,
    )
    peer.start()
    peer.wait_recv()
    mine = B[src] + RB[...]
    routed = jnp.dot(OH1[...], split3(mine), preferred_element_type=jnp.float32)
    for o in range(n_gy):
        S2[o] = routed[o * cap : (o + 1) * cap, :]
    sends = []
    for d in range(1, n_gy):
        o = lax.rem(gy + d, n_gy)
        sends.append(
            pltpu.make_async_remote_copy(
                S2.at[o], R2.at[gy], rt_s.at[d], rt_r.at[d],
                device_id={"gy": o}, device_id_type=MESH,
            )
        )
        sends[-1].start()
    R2[gy] = S2[gy]
    for c in sends:
        c.wait_recv()
    for o in range(n_gy):
        RF[o * cap : (o + 1) * cap, :] = R2[o]
    out[...] = jnp.dot(OH2[...], split3(RF[...]), preferred_element_type=jnp.float32)
    for c in sends:
        c.wait_send()
    peer.wait_send()


def tiled(state):
    lead = state.shape[:-2]
    x, yz = state.shape[-2:]
    n = len(lead)
    state = state.reshape(lead + (x // 8, 8, yz // 128, 128))
    return state.transpose(tuple(range(n)) + (n, n + 2, n + 1, n + 3))


def per_device(
    n_gx, n_gy, forward_state, adjoint_state, permittivity, waveform, source_cell,
    block_owner, block_slot, owner_rows,
):
    NS = forward_state.shape[0]
    X, YZ = permittivity.shape
    T = YZ // 128
    NB = block_owner.shape[0] * block_owner.shape[1]
    cap = max(2, (NB + n_gy - 1) // n_gy)
    cols = BX * BY * NZ // 2
    sims = 2 * NS
    f32 = jnp.float32
    dma = pltpu.SemaphoreType.DMA
    any_spec = pl.BlockSpec(memory_space=pl.ANY)
    vmem = pl.BlockSpec(memory_space=pltpu.VMEM)
    return pl.pallas_call(
        functools.partial(kernel, n_gx, n_gy, cap),
        out_shape=jax.ShapeDtypeStruct((NB, cols), f32),
        in_specs=[any_spec] * 8,
        out_specs=vmem,
        scratch_shapes=[
            pltpu.VMEM((sims, 6, T, X, 128), f32),
            pltpu.VMEM((T, X, 128), f32),
            pltpu.VMEM((sims, 2, X, 128), f32),
            pltpu.VMEM((sims, 2, X, 128), f32),
            pltpu.VMEM((sims, 3, T + 1, X + 8, 128), f32),
            pltpu.VMEM((sims, 3, T + 1, X + 8, 128), f32),
            pltpu.VMEM((T, X, 128), f32),
            pltpu.VMEM((NS, 2, 3, T, X, 128), f32),
            pltpu.VMEM((NS, 3, T, X, 128), f32),
            pltpu.VMEM((T, X, 128), f32),
            pltpu.VMEM((sims, CHUNKS, 2, T // CHUNKS, 128), f32),
            pltpu.VMEM((sims, CHUNKS, 2, T // CHUNKS, 128), f32),
            pltpu.VMEM((sims, CHUNKS, 2, T // CHUNKS, 128), f32),
            pltpu.VMEM((sims, CHUNKS, 2, T // CHUNKS, 128), f32),
            pltpu.VMEM((2, NB, cols), f32),
            pltpu.VMEM((NB, cols), f32),
            pltpu.VMEM((n_gy, cap, cols), f32),
            pltpu.VMEM((n_gy, cap, cols), f32),
            pltpu.VMEM((n_gy * cap, cols), f32),
            pltpu.VMEM((NB, 3 * NB), jnp.bfloat16),
            pltpu.VMEM((NB, 3 * NB), jnp.bfloat16),
            pltpu.SMEM(waveform.shape, f32),
            pltpu.SMEM(source_cell.shape, jnp.int32),
            pltpu.VMEM(block_owner.shape, jnp.int32),
            pltpu.VMEM(block_slot.shape, jnp.int32),
            pltpu.VMEM(owner_rows.shape, jnp.int32),
            dma((5,)),
            dma((sims, 2, X // 8)),
            dma((X // 8,)),
            dma((sims, CHUNKS)),
            dma((sims, CHUNKS)),
            dma((sims, CHUNKS)),
            dma((sims, CHUNKS)),
            dma((sims, 2)),
            dma((sims, 2)),
            dma((sims, 2)),
            dma((sims, 2)),
            dma((2,)),
            dma((n_gy,)),
            dma((n_gy,)),
        ],
        compiler_params=pltpu.CompilerParams(
            collective_id=0, has_side_effects=True, vmem_limit_bytes=62 * 1024 * 1024
        ),
    )(
        tiled(forward_state), tiled(adjoint_state), tiled(permittivity),
        waveform, source_cell, block_owner, block_slot, owner_rows,
    )


def solution(mesh):
    in_specs = (
        P("src", None, "gx", "gy"),
        P("src", None, "gx", "gy"),
        P("gx", "gy"),
        P("src", None),
        P("src", None),
        P("gx", "gy"),
        P("gx", "gy"),
        P(("gx", "gy"), None),
    )
    out_specs = P(("gx", "gy"), "src")
    sizes = dict(mesh.shape)
    return jax.shard_map(
        functools.partial(per_device, sizes["gx"], sizes["gy"]),
        mesh=mesh, in_specs=in_specs, out_specs=out_specs, check_vma=False,
    )
```
